512 devices in a mesh: gx: 16 (over y, core), gy: 32 (over x, z).
Axes of the slice: x: 4, y: 8, z: 8, core: 2. Of those that a mesh axis runs over, the one named last changes fastest.
Arguments:
- wave: float32 [2, 2, 256, 512, 256], P(None, None, 'gx', 'gy'), may hold values from -6 to 6
- atom_anchors: int32 [3, 16, 512], P(None, 'gx', 'gy'), may hold values from 0 to 511, as said below
- betas: float32 [16, 512, 8, 2304], P('gx', 'gy'), may hold values from -0.5 to 0.5
- couplings: float32 [16, 512, 8, 8], P('gx', 'gy'), may hold values from -2.5 to 2.5
- atom_counts: int32 [16, 32], P('gx', 'gy'), may hold values from 4 to 16, as said below
Outputs:
- advanced: float32 [2, 2, 256, 512, 256], P(None, None, 'gx', 'gy')
The draws below stay inside these ranges and needn't reach their ends.
Inputs may be any that keep to these rules, and one draw needn't show every extreme that they name: `atom_anchors`: slot k of domain (i, j) has its x coordinate in [i * 16, (i + 1) * 16), its y coordinate in [j * 16, (j + 1) * 16), and its z coordinate in [0, 240]. `atom_counts`: some domain has exactly 16 live slots and some exactly 4.
All inputs are finite; a program needn't handle non-finite values.
Results may differ from the reference program's by a relative error of at most 0.00011.
Values sent between devices are 32-bit elements; how exact they have to be, the bound alone decides.
No kernel may reach another device: no remote copies, remote signals or barrier semaphores. Data moves between devices by JAX's collectives and lax.ppermute only.
A program may use at most 128 MiB of HBM per device.

```python
import jax
import jax.numpy as jnp
from jax import lax

CX = 16
CY = 16
NZ = 256
A_DEV = 16
NB = 2
NPROJ = 8
BX = 12
BY = 12
BZ = 16
BOX = 2304
NX = 256
NY = 512
N_GX = 16
N_GY = 32


def draw_atom_anchors(key, part):
    key = jax.random.fold_in(key, 11)
    domain_rows = NX // CX
    domain_cols = NY // CY
    key_x, key_y, key_z = jax.random.split(key, 3)
    shape_atoms = (domain_rows, domain_cols * A_DEV)
    start_x = jax.random.randint(key_x, shape_atoms, 0, CX) + (jnp.arange(domain_rows) * CX)[:, None]
    start_y = jax.random.randint(key_y, shape_atoms, 0, CY) + (jnp.arange(domain_cols * A_DEV) // A_DEV * CY)[None, :]
    start_z = jax.random.randint(key_z, shape_atoms, 0, NZ - BZ + 1)
    start_x = start_x.at[0, 0].set(0).at[domain_rows - 1, domain_cols * A_DEV - 1].set(NX - 1)
    start_y = start_y.at[0, 0].set(0).at[domain_rows - 1, domain_cols * A_DEV - 1].set(NY - 1)
    start_z = start_z.at[0, 0].set(NZ - BZ).at[domain_rows - 1, domain_cols * A_DEV - 1].set(0)
    return jnp.stack([start_x, start_y, start_z]).astype(jnp.int32)


def draw_atom_counts(key, part):
    key = jax.random.fold_in(key, 17)
    domain_rows = NX // CX
    domain_cols = NY // CY
    domains = domain_rows * domain_cols
    key_one, key_two, key_three = jax.random.split(key, 3)
    top_extra = A_DEV - A_DEV // 4
    drawn = jax.random.randint(key_one, (domains,), 0, top_extra + 1)
    counts = A_DEV // 4 + drawn * drawn // max(top_extra, 1)
    full_index = jax.random.randint(key_two, (), 0, domains)
    low_index = (full_index + 1 + jax.random.randint(key_three, (), 0, domains - 1)) % domains
    all_index = jnp.arange(domains)
    counts = jnp.where(all_index == full_index, A_DEV, counts)
    counts = jnp.where(all_index == low_index, A_DEV // 4, counts)
    return counts.reshape(domain_rows, domain_cols).astype(jnp.int32)


def steps_of(rng, extent, pieces, least, high):
    factor_of, own = 1.0, jax.random.fold_in(rng, 6)
    for dim, blocks in pieces:
        heights = jnp.exp(jax.random.uniform(jax.random.fold_in(own, dim), (blocks,), jnp.float32, least / len(pieces), high / len(pieces)))
        factor_of = factor_of * jnp.repeat(heights, extent[dim] // blocks).reshape([-1 if axis == dim else 1 for axis in range(len(extent))])
    return factor_of


def gaussian(key, dims, scale, limit, cuts=(), kind=jnp.bfloat16):
    values = jax.random.normal(key, dims, jnp.float32) * scale
    if len(cuts) > 0:
        values = steps_of(key, dims, cuts, -0.22, 0.18) * values
    return jnp.clip(values, min=-limit, max=limit).astype(kind)


def setup_inputs(seed: int = 0) -> dict:
    key_of = jax.random.split(jax.random.key(seed), 6)
    wave = gaussian(key_of[0], (NB, 2, NX, NY, NZ), 1.0, 6.0, ((2, 16), (3, 32)), jnp.float32)
    atom_anchors = draw_atom_anchors(jax.random.fold_in(key_of[5], 71), 0)
    betas = gaussian(key_of[2], (N_GX, N_GY * A_DEV, NPROJ, BOX), (BX * BY) ** -0.5, 0.5, ((0, 16), (1, 32)), jnp.float32)
    couplings = gaussian(key_of[3], (N_GX, N_GY * A_DEV, NPROJ, NPROJ), 0.35, 2.5, ((0, 16), (1, 32)), jnp.float32)
    atom_counts = draw_atom_counts(jax.random.fold_in(key_of[5], 71), 0)
    return dict(wave=wave, atom_anchors=atom_anchors, betas=betas, couplings=couplings, atom_counts=atom_counts)


time_step = 0.5
highest = lax.Precision.HIGHEST


def extend(wave_field):
    wave_field = jnp.concatenate([wave_field, wave_field[:, :, :BX - 1]], axis=2)
    return jnp.concatenate([wave_field, wave_field[:, :, :, :BY - 1]], axis=3)


def fold(summed):
    inner = summed[:, :, :NX, :NY]
    inner = inner.at[:, :, :BX - 1].add(summed[:, :, NX:, :NY])
    inner = inner.at[:, :, :, :BY - 1].add(summed[:, :, :NX, NY:])
    return inner.at[:, :, :BX - 1, :BY - 1].add(summed[:, :, NX:, NY:])


def nonlocal_apply(wave_field, starts, flat_betas, flat_couplings, live_mask):
    region = extend(wave_field)
    leading = (wave_field.shape[0], wave_field.shape[1])
    box_shape = leading + (BX, BY, BZ)
    anchor_zero = jnp.zeros((), jnp.int32)

    def project(atom_item):
        box_start, projector = atom_item
        box_cells = lax.dynamic_slice(region, (anchor_zero, anchor_zero, box_start[0], box_start[1], box_start[2]), box_shape)
        box_cells = box_cells.reshape(leading[0] * leading[1], BX * BY * BZ)
        return jnp.dot(projector, box_cells.T, precision=highest)

    coeffs = lax.map(project, (starts, flat_betas))
    scaled = jnp.einsum("apq,aqv->apv", flat_couplings, coeffs, precision=highest) * live_mask[:, None, None]

    def add_one(number, summed):
        box_piece = jnp.dot(scaled[number].T, flat_betas[number], precision=highest).reshape(box_shape)
        box_index = (anchor_zero, anchor_zero, starts[number, 0], starts[number, 1], starts[number, 2])
        current = lax.dynamic_slice(summed, box_index, box_shape)
        return lax.dynamic_update_slice(summed, current + box_piece, box_index)

    summed = lax.fori_loop(0, starts.shape[0], add_one, jnp.zeros_like(region))
    return fold(summed)


def reference(wave, atom_anchors, betas, couplings, atom_counts):
    slots = atom_anchors.shape[2]
    starts = atom_anchors.reshape(3, -1).T.astype(jnp.int32)
    flat_betas = betas.reshape(-1, betas.shape[2], betas.shape[3])
    flat_couplings = couplings.reshape(-1, couplings.shape[2], couplings.shape[3])
    slot_index = jnp.arange(slots, dtype=jnp.int32) % A_DEV
    live_mask = (slot_index[None, :] < jnp.repeat(atom_counts, A_DEV, axis=1)).astype(wave.dtype).reshape(-1)
    first_term = nonlocal_apply(wave, starts, flat_betas, flat_couplings, live_mask)
    second_term = nonlocal_apply(first_term, starts, flat_betas, flat_couplings, live_mask)
    half_square = 0.5 * time_step * time_step
    real_part = wave[:, 0] + time_step * first_term[:, 1] - half_square * second_term[:, 0]
    imag_part = wave[:, 1] - time_step * first_term[:, 0] - half_square * second_term[:, 1]
    return jnp.stack([real_part, imag_part], axis=1)
```

```python
import functools

import jax
import jax.numpy as jnp
from jax import lax
from jax.experimental import pallas as pl
from jax.experimental.pallas import tpu as pltpu
from jax.sharding import PartitionSpec as P

BX = 12
BY = 12
BZ = 16
NP = 8
SLOTS = 16
CELLS = 16
PAD = 3
ROWS = 72
CHUNKS = ((0, 16),)
time_step = 0.5
half_square = 0.5 * time_step * time_step
f32 = jnp.float32

FIELD = (2, (CELLS + 2 * PAD) * ROWS, 128)
PLACED = (BX, 2, NP, 128)


def shift(block, axis, distance):
    n = lax.axis_size(axis)
    return lax.ppermute(block, axis, [(i, (i + distance) % n) for i in range(n)])


def iotas():
    row = lax.broadcasted_iota(jnp.int32, (8, 128), 0)
    lane = lax.broadcasted_iota(jnp.int32, (8, 128), 1)
    return row, lane


def exchange_blocks(tiles):
    row, lane = iotas()
    tiles = list(tiles)
    for d in (4, 2, 1):
        odd = (lane & (16 * d)) != 0
        for i in range(8):
            if i & d:
                continue
            a, b = tiles[i], tiles[i | d]
            tiles[i] = jnp.where(odd, pltpu.roll(b, 16 * d, 1), a)
            tiles[i | d] = jnp.where(odd, b, pltpu.roll(a, 128 - 16 * d, 1))
    return tiles


def field_rows(x, row):
    return pl.ds(x * ROWS + row, 8)


def load_field(plain, field):
    def part(step, carry):
        c, xb = step >> 1, step & 1
        for h in range(2):
            for k in range(2):
                tiles = [
                    plain[k, pl.ds(c * 256 + xb * 128 + 8 * h + i, 8, stride=16), :] for i in range(8)
                ]
                for i, tile in enumerate(exchange_blocks(tiles)):
                    start = (PAD + xb * 8) * ROWS + 32 * k + 4 * i + c
                    field[h, pl.ds(start, 8, stride=ROWS), :] = tile
        return carry

    lax.fori_loop(0, 8, part, 0)
    clear_rims(field)
    zero = jnp.zeros((8, 128), f32)
    for h in range(2):
        for x in range(CELLS):
            field[h, field_rows(PAD + x, 64), :] = zero


def add_field(plain, field):
    def part(step, carry):
        c, xb = step >> 1, step & 1
        for h in range(2):
            for k in range(2):
                tiles = [
                    field[h, pl.ds((PAD + xb * 8) * ROWS + 32 * k + 4 * i + c, 8, stride=ROWS), :]
                    for i in range(8)
                ]
                for i, tile in enumerate(exchange_blocks(tiles)):
                    at = pl.ds(c * 256 + xb * 128 + 8 * h + i, 8, stride=16)
                    plain[k, at, :] = plain[k, at, :] + tile
        return carry

    lax.fori_loop(0, 8, part, 0)


def clear_rims(field):
    zero = jnp.zeros((PAD * ROWS, 128), f32)
    for h in range(2):
        field[h, pl.ds(0, PAD * ROWS), :] = zero
        field[h, pl.ds((PAD + CELLS) * ROWS, PAD * ROWS), :] = zero


def clear_field(field):
    zero = jnp.zeros((ROWS, 128), f32)

    def plane(x, carry):
        for h in range(2):
            field[h, pl.ds(x * ROWS, ROWS), :] = zero
        return carry

    lax.fori_loop(0, CELLS + 2 * PAD, plane, 0)


def place(raw, raw_slot, placed, slot, dy, dz):
    row, lane = iotas()
    s = dz & 15
    amounts = {}
    for odd in range(2):
        for late in range(2):
            r = (dy * 16 + s - 16 * late - 64 * odd + 512) & 255
            q = r & 127
            flip = r > 127
            amounts[odd, late] = (q, jnp.logical_xor(lane < q, flip))
    keep = (lane & 15) >= s
    for u in range(BX):
        k = (3 * u) // 2
        a = raw[raw_slot, :, pl.ds(128 * k, 128)]
        b = raw[raw_slot, :, pl.ds(128 * k + 128, 128)]
        outs = []
        for late in range(2):
            q, from_b = amounts[u % 2, late]
            ra = pltpu.roll(a, q, 1)
            rb = pltpu.roll(b, q, 1)
            outs.append((jnp.where(from_b, rb, ra), jnp.where(from_b, ra, rb)))
        for h in range(2):
            placed[slot, u, h] = jnp.where(keep, outs[0][h], outs[1][h])


def masks(dy, dz, past_y):
    row, lane = iotas()
    s = dz & 15
    zl = lane & 15
    z_ok = jnp.logical_xor(zl < s, row < 4)
    result = []
    for h in range(2):
        y = (lane >> 4) + 8 * h
        if past_y:
            y_ok = y < dy + BY - CELLS
        else:
            y_ok = jnp.logical_and(y >= dy, y < dy + BY)
        result.append(jnp.logical_and(z_ok, y_ok))
    return result


def x_blocks(dx, past_x):
    if past_x:
        return (CELLS - dx) >> 2, 3, PAD + dx - CELLS
    return 0, jnp.minimum(3, (CELLS + 3 - dx) >> 2), PAD + dx


def project(placed, slot, field, dx, dy, dz, past_x, past_y):
    first, last, base = x_blocks(dx, past_x)
    mask = masks(dy, dz, past_y)
    rows = (dz >> 4) * 4

    def four(block, sums):
        sums = list(sums)
        for i in range(4):
            u = block * 4 + i
            for h in range(2):
                cells = field[h, field_rows(base + u, rows), :]
                cells = jnp.where(mask[h], cells, 0.0)
                for p in range(NP):
                    sums[p] = sums[p] + cells * placed[slot, u, h, pl.ds(p, 1), :]
        return tuple(sums)

    return lax.fori_loop(first, last, four, tuple(jnp.zeros((8, 128), f32) for _ in range(NP)))


def spread(placed, slot, field, scaled, dx, dy, dz, past_x, past_y):
    first, last, base = x_blocks(dx, past_x)
    mask = masks(dy, dz, past_y)
    rows = (dz >> 4) * 4

    def four(block, carry):
        at = [(i, h) for i in range(4) for h in range(2)]
        cells = [field[h, field_rows(base + block * 4 + i, rows), :] for i, h in at]
        sums = []
        for (i, h), old in zip(at, cells, strict=True):
            u = block * 4 + i
            total = scaled[0] * placed[slot, u, h, pl.ds(0, 1), :]
            for p in range(1, NP):
                total = total + scaled[p] * placed[slot, u, h, pl.ds(p, 1), :]
            sums.append(old + jnp.where(mask[h], total, 0.0))
        for (i, h), new in zip(at, sums, strict=True):
            field[h, field_rows(base + block * 4 + i, rows), :] = new
        return carry

    lax.fori_loop(first, last, four, 0)


def keep_sums(kept, slot, sums):
    for p in range(NP):
        kept[slot, p] = sums[p]


def pack(kept, slot, count):
    row, lane = iotas()

    def four(step, packed):
        for i in range(4):
            for p in range(NP):
                value = jnp.sum(kept[slot + 4 * step + i, p], axis=1, keepdims=True)
                packed = jnp.where(lane == (4 * step + i) * NP + p, value, packed)
        return packed

    return lax.fori_loop(0, (count + 3) >> 2, four, jnp.zeros((8, 128), f32))


def clear_sums(kept, slots):
    def one(slot, carry):
        kept[slot] = jnp.zeros((NP, 8, 128), f32)
        return carry

    lax.fori_loop(0, slots, one, 0, unroll=2)


def unpack(scaled, slot, columns, count):
    def four(step, carry):
        for i in range(4):
            for p in range(NP):
                index = jnp.full((8, 128), (4 * step + i) * NP + p, jnp.int32)
                columns[slot + 4 * step + i, p] = jnp.take_along_axis(
                    scaled, index, axis=1, mode="promise_in_bounds"
                )
        return carry

    lax.fori_loop(0, (count + 3) >> 2, four, 0)


def couple(coeffs, turned):
    row, lane = iotas()
    whole = coeffs + pltpu.roll(coeffs, 4, 0)
    matrix = jnp.concatenate([jnp.where((lane >> 3) == a, turned, 0.0) for a in range(SLOTS)], axis=0)
    return jnp.dot(whole, matrix, precision=lax.Precision.HIGHEST, preferred_element_type=f32)


def for_atoms(meta, group, past_x, past_y, first, count, body):
    at = group % 2 * 2 + group // 2
    stop = jnp.clip(meta[at, 48] - first, 0, count)

    def one(local, carry):
        atom = first + local
        dx, dy, dz = meta[at, atom], meta[at, 16 + atom], meta[at, 32 + atom]
        if not (past_x or past_y):
            body(local, atom, dx, dy, dz)
            return carry
        reach = dx > CELLS - BX if past_x else dy > CELLS - BY
        if past_x and past_y:
            reach = jnp.logical_and(reach, dy > CELLS - BY)

        @pl.when(reach)
        def _():
            body(local, atom, dx, dy, dz)

        return carry

    lax.fori_loop(0, stop, one, 0)


def copy_atom(ref, local, into, slot, sems):
    return pltpu.make_async_copy(ref.at[local], into.at[slot], sems.at[slot])


def copy_plain(wave_ref, plain, sems):
    return [
        pltpu.make_async_copy(wave_ref.at[:, pl.ds(128 * k, 128)], plain.at[k], sems.at[k])
        for k in range(2)
    ]


def near_kernel(
    meta, own, other, wave_ref, own_placed, other_placed, own_sums, other_sums,
    raw, plain, field, kept, sems, plain_sems,
):
    groups = ((0, own, own_placed, own_sums), (2, other, other_placed, other_sums))
    for copy in copy_plain(wave_ref, plain, plain_sems):
        copy.start()
    for group, ref, _, _ in groups:

        def begin(local, atom, dx, dy, dz, group=group, ref=ref):
            copy_atom(ref, local, raw, group * SLOTS + atom, sems).start()

        for_atoms(meta, group, 0, 0, 0, SLOTS, begin)
    clear_sums(kept, 2 * SLOTS)
    for copy in copy_plain(wave_ref, plain, plain_sems):
        copy.wait()
    load_field(plain, field)
    for group, ref, placed, sums_out in groups:
        past_x = group // 2

        def ready(local, atom, dx, dy, dz, group=group, ref=ref, placed=placed):
            slot = group * SLOTS + atom
            copy_atom(ref, local, raw, slot, sems).wait()
            place(raw, slot, placed, atom, dy, dz)

        def work(local, atom, dx, dy, dz, past_x=past_x, placed=placed, group_slot=past_x * SLOTS):
            sums = project(placed, atom, field, dx, dy, dz, past_x, 0)
            keep_sums(kept, group_slot + atom, sums)

        for_atoms(meta, group, 0, 0, 0, SLOTS, ready)
        for_atoms(meta, group, past_x, 0, 0, SLOTS, work)
        sums_out[...] = pack(kept, past_x * SLOTS, meta[past_x, 48])


def ahead_kernel(
    meta, own, other, wave_ref, own_before, other_before, own_sums, other_sums,
    placed, plain, field, kept, sems, plain_sems,
):
    groups = ((0, own, own_before, own_sums), (2, other, other_before, other_sums))
    for copy in copy_plain(wave_ref, plain, plain_sems):
        copy.start()
    for group, ref, _, _ in groups:

        def begin(local, atom, dx, dy, dz, group=group, ref=ref):
            copy_atom(ref, local, placed, group // 2 * SLOTS + atom, sems).start()

        for_atoms(meta, group, group // 2, 1, 0, SLOTS, begin)
    clear_sums(kept, 2 * SLOTS)
    for copy in copy_plain(wave_ref, plain, plain_sems):
        copy.wait()
    load_field(plain, field)
    for group, ref, before, sums_out in groups:

        def work(local, atom, dx, dy, dz, group=group, ref=ref):
            slot = group // 2 * SLOTS + atom
            copy_atom(ref, local, placed, slot, sems).wait()
            keep_sums(kept, slot, project(placed, slot, field, dx, dy, dz, group // 2, 1))

        for_atoms(meta, group, group // 2, 1, 0, SLOTS, work)
        sums_out[...] = before[...] + pack(kept, group // 2 * SLOTS, meta[group // 2, 48])


def place_kernel(first, count, meta, side, corner, side_placed, corner_placed, raw, sems):
    groups = ((1, side, side_placed), (3, corner, corner_placed))
    for group, ref, _ in groups:

        def begin(local, atom, dx, dy, dz, group=group, ref=ref):
            copy_atom(ref, local, raw, group // 2 * count + local, sems).start()

        for_atoms(meta, group, group // 2, 1, first, count, begin)
    for group, ref, placed in groups:

        def work(local, atom, dx, dy, dz, group=group, ref=ref, placed=placed):
            slot = group // 2 * count + local
            copy_atom(ref, local, raw, slot, sems).wait()
            place(raw, slot, placed, local, dy, dz)

        for_atoms(meta, group, group // 2, 1, first, count, work)


def parts_of():
    parts = [(0, 0, SLOTS), (2, 0, SLOTS)]
    for first, count in CHUNKS:
        parts += [(1, first, count), (3, first, count)]
    return parts


def begin_parts(meta, refs, placed, sems):
    for (group, first, count), ref in zip(parts_of(), refs, strict=True):

        def begin(local, atom, dx, dy, dz, group=group, ref=ref):
            copy_atom(ref, local, placed, group * SLOTS + atom, sems).start()

        for_atoms(meta, group, group // 2, group % 2, first, count, begin)


def spread_parts(meta, refs, placed, field, columns, sems):
    for (group, first, count), ref in zip(parts_of(), refs, strict=True):

        def work(local, atom, dx, dy, dz, group=group, ref=ref):
            slot = group * SLOTS + atom
            copy_atom(ref, local, placed, slot, sems).wait()
            scaled = [columns[slot, p] for p in range(NP)]
            spread(placed, slot, field, scaled, dx, dy, dz, group // 2, group % 2)

        for_atoms(meta, group, group // 2, group % 2, first, count, work)


def row_of(group):
    return group % 2 * 2 + group // 2


def second_kernel(meta, home, visit, coupling, *rest):
    n = len(parts_of())
    refs = rest[:n]
    scaled_out, low, high, field, placed, columns, kept, sems = rest[n:]
    begin_parts(meta, refs, placed, sems)
    clear_field(field)
    clear_sums(kept, 4 * SLOTS)
    for group in range(4):
        at = row_of(group)
        scaled = couple((home, visit)[group % 2][group // 2], coupling[at, pl.ds(0, 8), :])
        scaled_out[group] = scaled
        unpack(scaled, group * SLOTS, columns, meta[at, 48])
    spread_parts(meta, refs, placed, field, columns, sems)
    clear_rims(field)
    for group in range(4):

        def work(local, atom, dx, dy, dz, group=group):
            slot = group * SLOTS + atom
            keep_sums(kept, slot, project(placed, slot, field, dx, dy, dz, group // 2, group % 2))

        for_atoms(meta, group, group // 2, group % 2, 0, SLOTS, work)
    for group in range(4):
        (low, high)[group // 2][group % 2] = pack(kept, group * SLOTS, meta[row_of(group), 48])


def last_kernel(meta, near, far, near_in, far_in, first_scaled, coupling, wave_ref, *rest):
    n = len(parts_of())
    refs = rest[:n]
    out, field, placed, columns, plain, sems, plain_sems = rest[n:]
    begin_parts(meta, refs, placed, sems)
    for copy in copy_plain(wave_ref, plain, plain_sems):
        copy.start()
    clear_field(field)
    row, lane = iotas()
    for group in range(4):
        at = group // 2
        if group % 2:
            coeffs = far[at] + far_in[at]
        else:
            coeffs = near[at] + near_in[at]
        second = couple(coeffs, coupling[row_of(group), pl.ds(0, 8), :])
        first = first_scaled[group]
        turned = jnp.where((row & 1) == 0, pltpu.roll(first, 7, 0), -pltpu.roll(first, 1, 0))
        total = time_step * turned - half_square * second
        unpack(total, group * SLOTS, columns, meta[row_of(group), 48])
    spread_parts(meta, refs, placed, field, columns, sems)
    for copy in copy_plain(wave_ref, plain, plain_sems):
        copy.wait()
    add_field(plain, field)
    backs = [
        pltpu.make_async_copy(plain.at[k], out.at[:, pl.ds(128 * k, 128)], plain_sems.at[k])
        for k in range(2)
    ]
    for copy in backs:
        copy.start()
    for copy in backs:
        copy.wait()


SMEM = pl.BlockSpec(memory_space=pltpu.SMEM)
VMEM = pl.BlockSpec(memory_space=pltpu.VMEM)
HBM = pl.BlockSpec(memory_space=pl.ANY)
params = pltpu.CompilerParams(vmem_limit_bytes=40 << 20)
cost = pl.CostEstimate(flops=20_000_000, bytes_accessed=16_000_000, transcendentals=0)
DMA = pltpu.SemaphoreType.DMA
small = jax.ShapeDtypeStruct((8, 128), f32)
pair_of = jax.ShapeDtypeStruct((2, 8, 128), f32)
plain_scratch = pltpu.VMEM((2, 4 * CELLS * CELLS, 128), f32)
field_scratch = pltpu.VMEM(FIELD, f32)


def tiles_scratch(slots):
    return pltpu.VMEM((slots, NP, 8, 128), f32)


def raw_scratch(slots):
    return pltpu.VMEM((slots, NP, BX * BY * BZ), f32)


def placed_scratch(slots):
    return pltpu.VMEM((slots,) + PLACED, f32)


def placed_shape(slots):
    return jax.ShapeDtypeStruct((slots,) + PLACED, f32)


def near_coeffs(meta, own, other, wave):
    return pl.pallas_call(
        near_kernel,
        out_shape=[placed_shape(SLOTS), placed_shape(SLOTS), small, small],
        in_specs=[SMEM, HBM, HBM, HBM],
        out_specs=[VMEM] * 4,
        scratch_shapes=[
            raw_scratch(3 * SLOTS), plain_scratch, field_scratch, tiles_scratch(2 * SLOTS),
            DMA((3 * SLOTS,)), DMA((2,)),
        ],
        compiler_params=params,
        cost_estimate=cost,
        name="near_coeffs",
    )(meta, own, other, wave)


def ahead_coeffs(meta, own, other, wave, own_before, other_before):
    return pl.pallas_call(
        ahead_kernel,
        out_shape=[small, small],
        in_specs=[SMEM, HBM, HBM, HBM, VMEM, VMEM],
        out_specs=[VMEM] * 2,
        scratch_shapes=[
            placed_scratch(2 * SLOTS), plain_scratch, field_scratch, tiles_scratch(2 * SLOTS),
            DMA((2 * SLOTS,)), DMA((2,)),
        ],
        compiler_params=params,
        cost_estimate=cost,
        name="ahead_coeffs",
    )(meta, own, other, wave, own_before, other_before)


def place_part(first, count, meta, side, corner):
    return pl.pallas_call(
        functools.partial(place_kernel, first, count),
        out_shape=[placed_shape(count), placed_shape(count)],
        in_specs=[SMEM, HBM, HBM],
        out_specs=[VMEM] * 2,
        scratch_shapes=[raw_scratch(2 * count), DMA((2 * count,))],
        compiler_params=params,
        cost_estimate=cost,
        name="place_part",
    )(meta, side, corner)


def second_coeffs(meta, home, visit, coupling, boxes):
    return pl.pallas_call(
        second_kernel,
        out_shape=[jax.ShapeDtypeStruct((4, 8, 128), f32), pair_of, pair_of],
        in_specs=[SMEM] + [VMEM] * 3 + [HBM] * len(boxes),
        out_specs=[VMEM] * 3,
        scratch_shapes=[
            field_scratch, placed_scratch(4 * SLOTS), tiles_scratch(4 * SLOTS), tiles_scratch(4 * SLOTS),
            DMA((4 * SLOTS,)),
        ],
        compiler_params=params,
        cost_estimate=cost,
        name="second_coeffs",
    )(meta, home, visit, coupling, *boxes)


def advance(meta, near, far, near_in, far_in, first_scaled, coupling, wave, boxes):
    return pl.pallas_call(
        last_kernel,
        out_shape=jax.ShapeDtypeStruct(wave.shape, f32),
        in_specs=[SMEM] + [VMEM] * 6 + [HBM] * (1 + len(boxes)),
        out_specs=HBM,
        scratch_shapes=[
            field_scratch, placed_scratch(4 * SLOTS), tiles_scratch(4 * SLOTS), plain_scratch,
            DMA((4 * SLOTS,)), DMA((2,)),
        ],
        compiler_params=params,
        cost_estimate=cost,
        name="advance",
    )(meta, near, far, near_in, far_in, first_scaled, coupling, wave, *boxes)


def per_device(wave, atom_anchors, betas, couplings, atom_counts):
    plain = wave.reshape(4 * CELLS * CELLS, wave.shape[4])
    own = betas[0]

    side = shift(own, "gy", 1)
    ahead = shift(plain, "gy", -1)

    here = jnp.stack([lax.axis_index("gx") * CELLS, lax.axis_index("gy") * CELLS, 0])
    offsets = atom_anchors[:, 0] - here[:, None].astype(jnp.int32)
    live = (jnp.arange(SLOTS) < atom_counts[0, 0]).astype(f32)
    turned = jnp.transpose(couplings[0] * live[:, None, None], (2, 0, 1)).reshape(NP, SLOTS * NP)
    numbers = jnp.concatenate([offsets.reshape(48), atom_counts.reshape(1), jnp.zeros((79,), jnp.int32)])
    message = jnp.concatenate([turned, numbers.astype(f32)[None]])
    sheet = jnp.pad(message.reshape(1, 9 * 128), ((0, NP - 1), (0, BX * BY * BZ - 9 * 128)))
    other = shift(jnp.concatenate([own, sheet[None]]), "gx", 1)
    pair = jnp.stack([message, other[SLOTS, 0, : 9 * 128].reshape(9, 128)])
    meta_pair = pair[:, 8].astype(jnp.int32)

    own_placed, other_placed, own_sums, other_sums = near_coeffs(meta_pair, own, other, plain)
    side, own_sums, other_sums = lax.optimization_barrier((side, own_sums, other_sums))
    messages = jnp.concatenate([pair, shift(pair, "gy", 1)])
    meta = messages[:, 8].astype(jnp.int32)
    corner = shift(side, "gx", 1)
    own_sums, other_sums = ahead_coeffs(meta_pair, own_placed, other_placed, ahead, own_sums, other_sums)
    boxes = [own_placed, other_placed, *place_part(0, SLOTS, meta, side, corner)]
    home = jnp.stack([own_sums + shift(other_sums, "gx", -1), other_sums + shift(own_sums, "gx", 1)])
    visit = shift(home, "gy", 1)

    first_scaled, low, high = second_coeffs(meta, home, visit, messages, boxes)
    low_in = shift(high, "gx", -1)
    high_in = shift(low, "gx", 1)
    low, high = low + low_in, high + high_in
    near = jnp.stack([low[0], high[0]])
    far = jnp.stack([low[1], high[1]])
    near_in = shift(far, "gy", -1)
    far_in = shift(near, "gy", 1)
    out = advance(meta, near, far, near_in, far_in, first_scaled, messages, plain, boxes)
    return out.reshape(wave.shape)


def solution(mesh):
    return jax.shard_map(
        per_device,
        mesh=mesh,
        in_specs=(
            P(None, None, "gx", "gy", None),
            P(None, "gx", "gy"),
            P("gx", "gy", None, None),
            P("gx", "gy", None, None),
            P("gx", "gy"),
        ),
        out_specs=P(None, None, "gx", "gy", None),
        check_vma=False,
    )
```

```python
import functools

import jax
import jax.numpy as jnp
from jax import lax
from jax.experimental import pallas as pl
from jax.experimental.pallas import tpu as pltpu
from jax.sharding import PartitionSpec as P

BX = 12
BY = 12
BZ = 16
NP = 8
SLOTS = 16
CELLS = 16
PAD = 3
ROWS = 72
HALF = SLOTS // 2
PARTS = ((0, 0, SLOTS), (2, 0, SLOTS), (1, 0, HALF), (3, 0, HALF), (1, HALF, HALF), (3, HALF, HALF))
time_step = 0.5
half_square = 0.5 * time_step * time_step
f32 = jnp.float32

FIELD = (2, (CELLS + 2 * PAD) * ROWS, 128)
PLACED = (BX, 2, NP, 128)


def shift(block, axis, distance):
    n = lax.axis_size(axis)
    return lax.ppermute(block, axis, [(i, (i + distance) % n) for i in range(n)])


def iotas():
    row = lax.broadcasted_iota(jnp.int32, (8, 128), 0)
    lane = lax.broadcasted_iota(jnp.int32, (8, 128), 1)
    return row, lane


def exchange_blocks(tiles):
    row, lane = iotas()
    tiles = list(tiles)
    for d in (4, 2, 1):
        odd = (lane & (16 * d)) != 0
        for i in range(8):
            if i & d:
                continue
            a, b = tiles[i], tiles[i | d]
            tiles[i] = jnp.where(odd, pltpu.roll(b, 16 * d, 1), a)
            tiles[i | d] = jnp.where(odd, b, pltpu.roll(a, 128 - 16 * d, 1))
    return tiles


def field_rows(x, row):
    return pl.ds(x * ROWS + row, 8)


def load_field(tile_at, field):
    def part(step, carry):
        c, xb = step >> 1, step & 1
        for h in range(2):
            for k in range(2):
                tiles = [tile_at(k, c, xb, 8 * h + i) for i in range(8)]
                for i, tile in enumerate(exchange_blocks(tiles)):
                    start = (PAD + xb * 8) * ROWS + 32 * k + 4 * i + c
                    field[h, pl.ds(start, 8, stride=ROWS), :] = tile
        return carry

    lax.fori_loop(0, 8, part, 0)
    clear_rims(field)
    zero = jnp.zeros((8, 128), f32)
    for h in range(2):
        for x in range(CELLS):
            field[h, field_rows(PAD + x, 64), :] = zero


def add_field(plain, field):
    def part(step, carry):
        c, xb = step >> 1, step & 1
        for h in range(2):
            for k in range(2):
                tiles = [
                    field[h, pl.ds((PAD + xb * 8) * ROWS + 32 * k + 4 * i + c, 8, stride=ROWS), :]
                    for i in range(8)
                ]
                for i, tile in enumerate(exchange_blocks(tiles)):
                    at = pl.ds(c * 256 + xb * 128 + 8 * h + i, 8, stride=16)
                    plain[k, at, :] = plain[k, at, :] + tile
        return carry

    lax.fori_loop(0, 8, part, 0)


def clear_rims(field):
    zero = jnp.zeros((PAD * ROWS, 128), f32)
    for h in range(2):
        field[h, pl.ds(0, PAD * ROWS), :] = zero
        field[h, pl.ds((PAD + CELLS) * ROWS, PAD * ROWS), :] = zero


def clear_field(field):
    zero = jnp.zeros((ROWS, 128), f32)

    def plane(x, carry):
        for h in range(2):
            field[h, pl.ds(x * ROWS, ROWS), :] = zero
        return carry

    lax.fori_loop(0, CELLS + 2 * PAD, plane, 0)


def place(raw, raw_slot, placed, slot, dy, dz):
    row, lane = iotas()
    s = dz & 15
    amounts = {}
    for odd in range(2):
        for late in range(2):
            r = (dy * 16 + s - 16 * late - 64 * odd + 512) & 255
            q = r & 127
            flip = r > 127
            amounts[odd, late] = (q, jnp.logical_xor(lane < q, flip))
    keep = (lane & 15) >= s
    for u in range(BX):
        k = (3 * u) // 2
        a = raw[raw_slot, :, pl.ds(128 * k, 128)]
        b = raw[raw_slot, :, pl.ds(128 * k + 128, 128)]
        outs = []
        for late in range(2):
            q, from_b = amounts[u % 2, late]
            ra = pltpu.roll(a, q, 1)
            rb = pltpu.roll(b, q, 1)
            outs.append((jnp.where(from_b, rb, ra), jnp.where(from_b, ra, rb)))
        for h in range(2):
            placed[slot, u, h] = jnp.where(keep, outs[0][h], outs[1][h])


def masks(dy, dz, past_y):
    row, lane = iotas()
    s = dz & 15
    zl = lane & 15
    z_ok = jnp.logical_xor(zl < s, row < 4)
    result = []
    for h in range(2):
        y = (lane >> 4) + 8 * h
        if past_y:
            y_ok = y < dy + BY - CELLS
        else:
            y_ok = jnp.logical_and(y >= dy, y < dy + BY)
        result.append(jnp.logical_and(z_ok, y_ok))
    return result


def x_blocks(dx, past_x):
    if past_x:
        return (CELLS - dx) >> 2, 3, PAD + dx - CELLS
    return 0, jnp.minimum(3, (CELLS + 3 - dx) >> 2), PAD + dx


def project(placed, slot, field, dx, dy, dz, past_x, past_y):
    first, last, base = x_blocks(dx, past_x)
    mask = masks(dy, dz, past_y)
    rows = (dz >> 4) * 4

    def four(block, sums):
        sums = list(sums)
        for i in range(4):
            u = block * 4 + i
            for h in range(2):
                cells = field[h, field_rows(base + u, rows), :]
                cells = jnp.where(mask[h], cells, 0.0)
                for p in range(NP):
                    sums[p] = sums[p] + cells * placed[slot, u, h, pl.ds(p, 1), :]
        return tuple(sums)

    return lax.fori_loop(first, last, four, tuple(jnp.zeros((8, 128), f32) for _ in range(NP)))


def spread(placed, slot, field, scaled, dx, dy, dz, past_x, past_y):
    first, last, base = x_blocks(dx, past_x)
    mask = masks(dy, dz, past_y)
    rows = (dz >> 4) * 4

    def four(block, carry):
        at = [(i, h) for i in range(4) for h in range(2)]
        cells = [field[h, field_rows(base + block * 4 + i, rows), :] for i, h in at]
        sums = []
        for (i, h), old in zip(at, cells, strict=True):
            u = block * 4 + i
            total = scaled[0] * placed[slot, u, h, pl.ds(0, 1), :]
            for p in range(1, NP):
                total = total + scaled[p] * placed[slot, u, h, pl.ds(p, 1), :]
            sums.append(old + jnp.where(mask[h], total, 0.0))
        for (i, h), new in zip(at, sums, strict=True):
            field[h, field_rows(base + block * 4 + i, rows), :] = new
        return carry

    lax.fori_loop(first, last, four, 0)


def keep_sums(kept, slot, sums):
    row, lane = iotas()
    for q in range(NP // 2):
        even, odd = sums[2 * q], sums[2 * q + 1]
        other = pltpu.roll(jnp.where(row < 4, odd, even), 4, 0)
        kept[slot, q] = jnp.where(row < 4, even, odd) + other


def pack(kept, slot, count):
    row, lane = iotas()
    pair = jnp.where((lane & 1) == (row >> 2), lane >> 1, -1)

    def four(step, packed):
        for i in range(4):
            for q in range(NP // 2):
                value = jnp.sum(kept[slot + 4 * step + i, q], axis=1, keepdims=True)
                packed = jnp.where(pair == (4 * step + i) * (NP // 2) + q, value, packed)
        return packed

    return lax.fori_loop(0, (count + 3) >> 2, four, jnp.zeros((8, 128), f32))


def clear_sums(kept, slots):
    def one(slot, carry):
        kept[slot] = jnp.zeros((NP // 2, 8, 128), f32)
        return carry

    lax.fori_loop(0, slots, one, 0, unroll=2)


def unpack(scaled, atom):
    return [
        jnp.take_along_axis(
            scaled, jnp.full((8, 128), atom * NP + p, jnp.int32), axis=1, mode="promise_in_bounds"
        )
        for p in range(NP)
    ]


def couple(coeffs, turned):
    row, lane = iotas()
    whole = coeffs + pltpu.roll(coeffs, 4, 0)
    matrix = jnp.concatenate([jnp.where((lane >> 3) == a, turned, 0.0) for a in range(SLOTS)], axis=0)
    return jnp.dot(whole, matrix, precision=lax.Precision.HIGHEST, preferred_element_type=f32)


def row_of(group):
    return group % 2 * 2 + group // 2


def for_atoms(meta, group, past_x, past_y, body, first=0, count=SLOTS):
    at = row_of(group)
    stop = jnp.minimum(meta[at, 48], first + count)

    def one(atom, carry):
        dx, dy, dz = meta[at, atom], meta[at, 16 + atom], meta[at, 32 + atom]
        if not (past_x or past_y):
            body(atom, dx, dy, dz)
            return carry
        reach = dx > CELLS - BX if past_x else dy > CELLS - BY
        if past_x and past_y:
            reach = jnp.logical_and(reach, dy > CELLS - BY)

        @pl.when(reach)
        def _():
            body(atom, dx, dy, dz)

        return carry

    lax.fori_loop(first, stop, one, 0)


def copy_atom(ref, local, into, slot, sems):
    return pltpu.make_async_copy(ref.at[local], into.at[slot], sems.at[slot])


def copy_plain(wave_ref, plain, sems):
    return [
        pltpu.make_async_copy(wave_ref.at[:, pl.ds(128 * k, 128)], plain.at[k], sems.at[k])
        for k in range(2)
    ]


def copy_front(wave_ref, plain, sems):
    return [
        pltpu.make_async_copy(wave_ref.at[:, :, pl.ds(128 * k, 128)], plain.at[k], sems.at[k])
        for k in range(2)
    ]


def near_kernel(
    meta, own, lower, upper, wave_ref, own_placed, other_placed, own_sums, other_sums,
    raw, plain, field, kept, sems, plain_sems,
):
    groups = ((0, own_placed, own_sums), (2, other_placed, other_sums))
    for copy in copy_plain(wave_ref, plain, plain_sems):
        copy.start()
    parts = ((0, own, 0, SLOTS, 0), (2, lower, 0, HALF, 1), (2, upper, HALF, HALF, 0))
    for group, ref, first, count, skip in parts:

        def begin(atom, dx, dy, dz, group=group, ref=ref, back=skip - first):
            copy_atom(ref, atom + back, raw, group // 2 * SLOTS + atom, sems).start()

        for_atoms(meta, group, 0, 0, begin, first, count)
    clear_sums(kept, 2 * SLOTS)
    for copy in copy_plain(wave_ref, plain, plain_sems):
        copy.wait()
    load_field(lambda k, c, xb, y: plain[k, pl.ds(c * 256 + xb * 128 + y, 8, stride=16), :], field)
    for group, placed, sums_out in groups:
        past_x = group // 2

        def ready(atom, dx, dy, dz, past_x=past_x, placed=placed):
            slot = past_x * SLOTS + atom
            copy_atom(own, atom, raw, slot, sems).wait()
            place(raw, slot, placed, atom, dy, dz)

        def work(atom, dx, dy, dz, past_x=past_x, placed=placed):
            sums = project(placed, atom, field, dx, dy, dz, past_x, 0)
            keep_sums(kept, past_x * SLOTS + atom, sums)

        for_atoms(meta, group, 0, 0, ready)
        for_atoms(meta, group, past_x, 0, work)
        sums_out[...] = pack(kept, past_x * SLOTS, meta[past_x, 48])


def ahead_kernel(
    meta, own, other, wave_ref, own_before, other_before, own_sums, other_sums,
    plain, field, kept, plain_sems,
):
    groups = ((0, own, own_before, own_sums), (2, other, other_before, other_sums))
    for copy in copy_front(wave_ref, plain, plain_sems):
        copy.start()
    clear_sums(kept, 2 * SLOTS)
    for copy in copy_front(wave_ref, plain, plain_sems):
        copy.wait()

    def tile_at(k, c, xb, y):
        if y >= BY - 1:
            return jnp.zeros((8, 128), f32)
        return plain[k, y, pl.ds(c * CELLS + xb * 8, 8), :]

    load_field(tile_at, field)
    for group, placed, before, sums_out in groups:

        def work(atom, dx, dy, dz, group=group, placed=placed):
            sums = project(placed, atom, field, dx, dy, dz, group // 2, 1)
            keep_sums(kept, group // 2 * SLOTS + atom, sums)

        for_atoms(meta, group, group // 2, 1, work)
        sums_out[...] = before[...] + pack(kept, group // 2 * SLOTS, meta[group // 2, 48])


def place_kernel(first, skip, meta, side, corner, side_placed, corner_placed, raw, sems):
    groups = ((1, side, side_placed), (3, corner, corner_placed))
    for group, ref, _ in groups:

        def begin(atom, dx, dy, dz, group=group, ref=ref):
            slot = group // 2 * HALF + atom - first
            copy_atom(ref, atom - first + skip, raw, slot, sems).start()

        for_atoms(meta, group, group // 2, 1, begin, first, HALF)
    for group, ref, placed in groups:

        def work(atom, dx, dy, dz, group=group, ref=ref, placed=placed):
            slot = group // 2 * HALF + atom - first
            copy_atom(ref, atom - first + skip, raw, slot, sems).wait()
            place(raw, slot, placed, atom - first, dy, dz)

        for_atoms(meta, group, group // 2, 1, work, first, HALF)


def spread_parts(meta, boxes, field, values):
    for (group, first, count), placed in zip(PARTS, boxes, strict=True):

        def work(atom, dx, dy, dz, group=group, first=first, placed=placed):
            scaled = unpack(values[group], atom)
            spread(placed, atom - first, field, scaled, dx, dy, dz, group // 2, group % 2)

        for_atoms(meta, group, group // 2, group % 2, work, first, count)


def second_kernel(meta, home, visit, coupling, *rest):
    boxes = rest[: len(PARTS)]
    scaled_out, low, high, field, kept = rest[len(PARTS) :]
    clear_field(field)
    clear_sums(kept, 4 * SLOTS)
    for group in range(4):
        matrix = coupling[row_of(group), pl.ds(0, 8), :]
        scaled_out[group] = couple((home, visit)[group % 2][group // 2], matrix)
    spread_parts(meta, boxes, field, scaled_out)
    clear_rims(field)
    for (group, first, count), placed in zip(PARTS, boxes, strict=True):

        def work(atom, dx, dy, dz, group=group, first=first, placed=placed):
            sums = project(placed, atom - first, field, dx, dy, dz, group // 2, group % 2)
            keep_sums(kept, group * SLOTS + atom, sums)

        for_atoms(meta, group, group // 2, group % 2, work, first, count)
    for group in range(4):
        packed = pack(kept, group * SLOTS, meta[row_of(group), 48])
        (low, high)[group // 2][group % 2] = packed


def last_kernel(meta, near, far, near_in, far_in, first_scaled, coupling, wave_ref, *rest):
    boxes = rest[: len(PARTS)]
    out, field, totals, plain, plain_sems = rest[len(PARTS) :]
    for copy in copy_plain(wave_ref, plain, plain_sems):
        copy.start()
    clear_field(field)
    row, lane = iotas()
    for group in range(4):
        at = group // 2
        if group % 2:
            coeffs = far[at] + far_in[at]
        else:
            coeffs = near[at] + near_in[at]
        second = couple(coeffs, coupling[row_of(group), pl.ds(0, 8), :])
        first = first_scaled[group]
        turned = jnp.where((row & 1) == 0, pltpu.roll(first, 7, 0), -pltpu.roll(first, 1, 0))
        totals[group] = time_step * turned - half_square * second
    spread_parts(meta, boxes, field, totals)
    for copy in copy_plain(wave_ref, plain, plain_sems):
        copy.wait()
    add_field(plain, field)
    backs = [
        pltpu.make_async_copy(plain.at[k], out.at[:, pl.ds(128 * k, 128)], plain_sems.at[k])
        for k in range(2)
    ]
    for copy in backs:
        copy.start()
    for copy in backs:
        copy.wait()


SMEM = pl.BlockSpec(memory_space=pltpu.SMEM)
VMEM = pl.BlockSpec(memory_space=pltpu.VMEM)
HBM = pl.BlockSpec(memory_space=pl.ANY)
params = pltpu.CompilerParams(vmem_limit_bytes=16 << 20)
cost = pl.CostEstimate(flops=20_000_000, bytes_accessed=16_000_000, transcendentals=0)
DMA = pltpu.SemaphoreType.DMA
small = jax.ShapeDtypeStruct((8, 128), f32)
pair_of = jax.ShapeDtypeStruct((2, 8, 128), f32)
plain_scratch = pltpu.VMEM((2, 4 * CELLS * CELLS, 128), f32)
front_scratch = pltpu.VMEM((2, BY - 1, 4 * CELLS, 128), f32)
field_scratch = pltpu.VMEM(FIELD, f32)


def tiles_scratch(slots):
    return pltpu.VMEM((slots, NP // 2, 8, 128), f32)


def raw_scratch(slots):
    return pltpu.VMEM((slots, NP, BX * BY * BZ), f32)


def placed_shape(slots):
    return jax.ShapeDtypeStruct((slots,) + PLACED, f32)


def call(body, name, out_shape, in_specs, out_specs, scratch):
    return pl.pallas_call(
        body,
        out_shape=out_shape,
        in_specs=in_specs,
        out_specs=out_specs,
        scratch_shapes=scratch,
        compiler_params=params,
        cost_estimate=cost,
        name=name,
    )


def near_coeffs(meta, own, lower, upper, wave):
    scratch = [raw_scratch(2 * SLOTS), plain_scratch, field_scratch, tiles_scratch(2 * SLOTS)]
    scratch += [DMA((2 * SLOTS,)), DMA((2,))]
    shapes = [placed_shape(SLOTS), placed_shape(SLOTS), small, small]
    run = call(near_kernel, "near_coeffs", shapes, [SMEM] + [HBM] * 4, [VMEM] * 4, scratch)
    return run(meta, own, lower, upper, wave)


def ahead_coeffs(meta, own, other, wave, own_before, other_before):
    scratch = [front_scratch, field_scratch, tiles_scratch(2 * SLOTS), DMA((2,))]
    specs = [SMEM, VMEM, VMEM, HBM, VMEM, VMEM]
    run = call(ahead_kernel, "ahead_coeffs", [small, small], specs, [VMEM] * 2, scratch)
    return run(meta, own, other, wave, own_before, other_before)


def place_behind(first, skip, meta, side, corner):
    scratch = [raw_scratch(2 * HALF), DMA((2 * HALF,))]
    shapes = [placed_shape(HALF), placed_shape(HALF)]
    body = functools.partial(place_kernel, first, skip)
    run = call(body, "place_behind", shapes, [SMEM, HBM, HBM], [VMEM] * 2, scratch)
    return run(meta, side, corner)


def second_coeffs(meta, home, visit, coupling, boxes):
    scratch = [field_scratch, tiles_scratch(4 * SLOTS)]
    shapes = [jax.ShapeDtypeStruct((4, 8, 128), f32), pair_of, pair_of]
    run = call(second_kernel, "second_coeffs", shapes, [SMEM] + [VMEM] * (3 + len(PARTS)), [VMEM] * 3, scratch)
    return run(meta, home, visit, coupling, *boxes)


def advance(meta, near, far, near_in, far_in, first_scaled, coupling, wave, boxes):
    scratch = [field_scratch, pltpu.VMEM((4, 8, 128), f32), plain_scratch, DMA((2,))]
    shape = jax.ShapeDtypeStruct(wave.shape, f32)
    specs = [SMEM] + [VMEM] * 6 + [HBM] + [VMEM] * len(PARTS)
    run = call(last_kernel, "advance", shape, specs, HBM, scratch)
    return run(meta, near, far, near_in, far_in, first_scaled, coupling, wave, *boxes)


def per_device(wave, atom_anchors, betas, couplings, atom_counts):
    plain = wave.reshape(4 * CELLS * CELLS, wave.shape[4])
    own = betas[0]

    front = wave.reshape(4 * CELLS, CELLS, wave.shape[4])[:, : BY - 1]
    ahead = shift(jnp.transpose(front, (1, 0, 2)), "gy", -1)

    here = jnp.stack([lax.axis_index("gx") * CELLS, lax.axis_index("gy") * CELLS, 0])
    offsets = atom_anchors[:, 0] - here[:, None].astype(jnp.int32)
    live = (jnp.arange(SLOTS) < atom_counts[0, 0]).astype(f32)
    turned = jnp.transpose(couplings[0] * live[:, None, None], (2, 0, 1)).reshape(NP, SLOTS * NP)
    numbers = jnp.concatenate([offsets.reshape(48), atom_counts.reshape(1), jnp.zeros((79,), jnp.int32)])
    message = jnp.concatenate([turned, numbers.astype(f32)[None]])
    sheet = jnp.pad(message.reshape(1, 9 * 128), ((0, NP - 1), (0, BX * BY * BZ - 9 * 128)))
    halves = [jnp.concatenate([sheet[None], own[:HALF]]), own[HALF:]]
    side = [shift(half, "gy", 1) for half in halves]
    other = [shift(half, "gx", 1) for half in halves]

    def sent(part):
        return part[0, 0, : 9 * 128].reshape(9, 128)

    pair = jnp.stack([message, sent(other[0])])
    meta_pair = pair[:, 8].astype(jnp.int32)

    own_placed, other_placed, own_sums, other_sums = near_coeffs(meta_pair, own, *other, plain)
    lower, own_sums = lax.optimization_barrier((side[0], own_sums))
    corner_lower = shift(lower, "gx", 1)
    messages = jnp.concatenate([pair, sent(lower)[None], sent(corner_lower)[None]])
    meta = messages[:, 8].astype(jnp.int32)
    own_sums, other_sums = ahead_coeffs(meta_pair, own_placed, other_placed, ahead, own_sums, other_sums)
    home = jnp.stack([own_sums + shift(other_sums, "gx", -1), other_sums + shift(own_sums, "gx", 1)])
    upper, home = lax.optimization_barrier((side[1], home))
    corner_upper = shift(upper, "gx", 1)
    boxes = [own_placed, other_placed]
    boxes += place_behind(0, 1, meta, lower, corner_lower)
    boxes += place_behind(HALF, 0, meta, upper, corner_upper)
    visit = shift(home, "gy", 1)

    first_scaled, low, high = second_coeffs(meta, home, visit, messages, boxes)
    low_in = shift(high, "gx", -1)
    high_in = shift(low, "gx", 1)
    low, high = low + low_in, high + high_in
    near = jnp.stack([low[0], high[0]])
    far = jnp.stack([low[1], high[1]])
    near_in = shift(far, "gy", -1)
    far_in = shift(near, "gy", 1)
    out = advance(meta, near, far, near_in, far_in, first_scaled, messages, plain, boxes)
    return out.reshape(wave.shape)


def solution(mesh):
    return jax.shard_map(
        per_device,
        mesh=mesh,
        in_specs=(
            P(None, None, "gx", "gy", None),
            P(None, "gx", "gy"),
            P("gx", "gy", None, None),
            P("gx", "gy", None, None),
            P("gx", "gy"),
        ),
        out_specs=P(None, None, "gx", "gy", None),
        check_vma=False,
    )
```

```python
import functools

import jax
import jax.numpy as jnp
from jax import lax
from jax.experimental import pallas as pl
from jax.experimental.pallas import tpu as pltpu
from jax.sharding import PartitionSpec as P

BX = 12
BY = 12
BZ = 16
NP = 8
SLOTS = 16
CELLS = 16
PAD = 3
ROWS = 72
HALF = SLOTS // 2
PARTS = ((0, 0, SLOTS), (2, 0, SLOTS), (1, 0, HALF), (3, 0, HALF), (1, HALF, HALF), (3, HALF, HALF))
time_step = 0.5
half_square = 0.5 * time_step * time_step
f32 = jnp.float32

FIELD = (2, (CELLS + 2 * PAD) * ROWS, 128)
PLACED = (BX, 2, NP, 128)
ATOM_ROWS = BX * BY * BZ * NP // 128
HEAD_ROWS = 16


def shift(block, axis, distance):
    n = lax.axis_size(axis)
    return lax.ppermute(block, axis, [(i, (i + distance) % n) for i in range(n)])


def iotas():
    row = lax.broadcasted_iota(jnp.int32, (8, 128), 0)
    lane = lax.broadcasted_iota(jnp.int32, (8, 128), 1)
    return row, lane


def exchange_blocks(tiles):
    row, lane = iotas()
    tiles = list(tiles)
    for d in (4, 2, 1):
        odd = (lane & (16 * d)) != 0
        for i in range(8):
            if i & d:
                continue
            a, b = tiles[i], tiles[i | d]
            tiles[i] = jnp.where(odd, pltpu.roll(b, 16 * d, 1), a)
            tiles[i | d] = jnp.where(odd, b, pltpu.roll(a, 128 - 16 * d, 1))
    return tiles


def field_rows(x, row):
    return pl.ds(x * ROWS + row, 8)


def load_field(tile_at, field):
    def part(step, carry):
        c, xb = step >> 1, step & 1
        for h in range(2):
            for k in range(2):
                tiles = [tile_at(k, c, xb, 8 * h + i) for i in range(8)]
                for i, tile in enumerate(exchange_blocks(tiles)):
                    start = (PAD + xb * 8) * ROWS + 32 * k + 4 * i + c
                    field[h, pl.ds(start, 8, stride=ROWS), :] = tile
        return carry

    lax.fori_loop(0, 8, part, 0)
    clear_rims(field)
    zero = jnp.zeros((8, 128), f32)
    for h in range(2):
        for x in range(CELLS):
            field[h, field_rows(PAD + x, 64), :] = zero


def add_field(plain, field):
    def part(step, carry):
        c, xb = step >> 1, step & 1
        for h in range(2):
            for k in range(2):
                tiles = [
                    field[h, pl.ds((PAD + xb * 8) * ROWS + 32 * k + 4 * i + c, 8, stride=ROWS), :]
                    for i in range(8)
                ]
                for i, tile in enumerate(exchange_blocks(tiles)):
                    at = pl.ds(c * 256 + xb * 128 + 8 * h + i, 8, stride=16)
                    plain[k, at, :] = plain[k, at, :] + tile
        return carry

    lax.fori_loop(0, 8, part, 0)


def clear_rims(field):
    zero = jnp.zeros((PAD * ROWS, 128), f32)
    for h in range(2):
        field[h, pl.ds(0, PAD * ROWS), :] = zero
        field[h, pl.ds((PAD + CELLS) * ROWS, PAD * ROWS), :] = zero


def clear_field(field):
    zero = jnp.zeros((ROWS, 128), f32)

    def plane(x, carry):
        for h in range(2):
            field[h, pl.ds(x * ROWS, ROWS), :] = zero
        return carry

    lax.fori_loop(0, CELLS + 2 * PAD, plane, 0)


def place(raw, raw_slot, placed, slot, dy, dz):
    row, lane = iotas()
    s = dz & 15
    amounts = {}
    for odd in range(2):
        for late in range(2):
            r = (dy * 16 + s - 16 * late - 64 * odd + 512) & 255
            q = r & 127
            flip = r > 127
            amounts[odd, late] = (q, jnp.logical_xor(lane < q, flip))
    keep = (lane & 15) >= s
    for u in range(BX):
        k = (3 * u) // 2
        a = raw[raw_slot, pl.ds(NP * k, NP), :]
        b = raw[raw_slot, pl.ds(NP * k + NP, NP), :]
        outs = []
        for late in range(2):
            q, from_b = amounts[u % 2, late]
            ra = pltpu.roll(a, q, 1)
            rb = pltpu.roll(b, q, 1)
            outs.append((jnp.where(from_b, rb, ra), jnp.where(from_b, ra, rb)))
        for h in range(2):
            placed[slot, u, h] = jnp.where(keep, outs[0][h], outs[1][h])


def masks(dy, dz, past_y):
    row, lane = iotas()
    s = dz & 15
    zl = lane & 15
    z_ok = jnp.logical_xor(zl < s, row < 4)
    result = []
    for h in range(2):
        y = (lane >> 4) + 8 * h
        if past_y:
            y_ok = y < dy + BY - CELLS
        else:
            y_ok = jnp.logical_and(y >= dy, y < dy + BY)
        result.append(jnp.logical_and(z_ok, y_ok))
    return result


def x_blocks(dx, past_x):
    if past_x:
        return (CELLS - dx) >> 2, 3, PAD + dx - CELLS
    return 0, jnp.minimum(3, (CELLS + 3 - dx) >> 2), PAD + dx


def project(placed, slot, field, dx, dy, dz, past_x, past_y):
    first, last, base = x_blocks(dx, past_x)
    mask = masks(dy, dz, past_y)
    rows = (dz >> 4) * 4

    def four(block, sums):
        sums = list(sums)
        for i in range(4):
            u = block * 4 + i
            for h in range(2):
                cells = field[h, field_rows(base + u, rows), :]
                cells = jnp.where(mask[h], cells, 0.0)
                for p in range(NP):
                    sums[p] = sums[p] + cells * placed[slot, u, h, pl.ds(p, 1), :]
        return tuple(sums)

    return lax.fori_loop(first, last, four, tuple(jnp.zeros((8, 128), f32) for _ in range(NP)))


def spread(placed, slot, field, scaled, dx, dy, dz, past_x, past_y):
    first, last, base = x_blocks(dx, past_x)
    mask = masks(dy, dz, past_y)
    rows = (dz >> 4) * 4

    def four(block, carry):
        at = [(i, h) for i in range(4) for h in range(2)]
        cells = [field[h, field_rows(base + block * 4 + i, rows), :] for i, h in at]
        sums = []
        for (i, h), old in zip(at, cells, strict=True):
            u = block * 4 + i
            total = scaled[0] * placed[slot, u, h, pl.ds(0, 1), :]
            for p in range(1, NP):
                total = total + scaled[p] * placed[slot, u, h, pl.ds(p, 1), :]
            sums.append(old + jnp.where(mask[h], total, 0.0))
        for (i, h), new in zip(at, sums, strict=True):
            field[h, field_rows(base + block * 4 + i, rows), :] = new
        return carry

    lax.fori_loop(first, last, four, 0)


def keep_sums(kept, slot, sums):
    row, lane = iotas()
    for q in range(NP // 2):
        even, odd = sums[2 * q], sums[2 * q + 1]
        other = pltpu.roll(jnp.where(row < 4, odd, even), 4, 0)
        kept[slot, q] = jnp.where(row < 4, even, odd) + other


def pack(kept, slot, count):
    row, lane = iotas()
    pair = jnp.where((lane & 1) == (row >> 2), lane >> 1, -1)

    def four(step, packed):
        for i in range(4):
            for q in range(NP // 2):
                value = jnp.sum(kept[slot + 4 * step + i, q], axis=1, keepdims=True)
                packed = jnp.where(pair == (4 * step + i) * (NP // 2) + q, value, packed)
        return packed

    return lax.fori_loop(0, (count + 3) >> 2, four, jnp.zeros((8, 128), f32))


def clear_sums(kept, slots):
    def one(slot, carry):
        kept[slot] = jnp.zeros((NP // 2, 8, 128), f32)
        return carry

    lax.fori_loop(0, slots, one, 0, unroll=2)


def unpack(scaled, atom):
    return [
        jnp.take_along_axis(
            scaled, jnp.full((8, 128), atom * NP + p, jnp.int32), axis=1, mode="promise_in_bounds"
        )
        for p in range(NP)
    ]


def couple(coeffs, turned):
    row, lane = iotas()
    whole = coeffs + pltpu.roll(coeffs, 4, 0)
    matrix = jnp.concatenate([jnp.where((lane >> 3) == a, turned, 0.0) for a in range(SLOTS)], axis=0)
    return jnp.dot(whole, matrix, precision=lax.Precision.HIGHEST, preferred_element_type=f32)


def row_of(group):
    return group % 2 * 2 + group // 2


def for_atoms(meta, group, past_x, past_y, body, first=0, count=SLOTS):
    at = row_of(group)
    stop = jnp.minimum(meta[at, 48], first + count)

    def one(atom, carry):
        dx, dy, dz = meta[at, atom], meta[at, 16 + atom], meta[at, 32 + atom]
        if not (past_x or past_y):
            body(atom, dx, dy, dz)
            return carry
        reach = dx > CELLS - BX if past_x else dy > CELLS - BY
        if past_x and past_y:
            reach = jnp.logical_and(reach, dy > CELLS - BY)

        @pl.when(reach)
        def _():
            body(atom, dx, dy, dz)

        return carry

    lax.fori_loop(first, stop, one, 0)


def copy_atom(ref, skip, local, into, slot, sems):
    rows = pl.ds(local * ATOM_ROWS + skip, ATOM_ROWS)
    return pltpu.make_async_copy(ref.at[rows], into.at[slot], sems.at[slot])


def copy_plain(wave_ref, plain, sems):
    return [
        pltpu.make_async_copy(wave_ref.at[:, pl.ds(128 * k, 128)], plain.at[k], sems.at[k])
        for k in range(2)
    ]


def copy_front(wave_ref, plain, sems):
    return [
        pltpu.make_async_copy(wave_ref.at[:, :, pl.ds(128 * k, 128)], plain.at[k], sems.at[k])
        for k in range(2)
    ]


def near_kernel(
    meta, own_lower, own_upper, lower, upper, wave_ref, own_placed, other_placed, own_sums, other_sums,
    raw, plain, field, kept, sems, plain_sems,
):
    groups = ((0, own_placed, own_sums), (2, other_placed, other_sums))
    for copy in copy_plain(wave_ref, plain, plain_sems):
        copy.start()
    for group, refs in ((0, (own_lower, own_upper)), (2, (lower, upper))):
        for first, skip, ref in ((0, HEAD_ROWS, refs[0]), (HALF, 0, refs[1])):

            def begin(atom, dx, dy, dz, group=group, first=first, skip=skip, ref=ref):
                slot = group // 2 * SLOTS + atom
                copy_atom(ref, skip, atom - first, raw, slot, sems).start()

            for_atoms(meta, group, 0, 0, begin, first, HALF)
    clear_sums(kept, 2 * SLOTS)
    for copy in copy_plain(wave_ref, plain, plain_sems):
        copy.wait()
    load_field(lambda k, c, xb, y: plain[k, pl.ds(c * 256 + xb * 128 + y, 8, stride=16), :], field)
    for group, placed, sums_out in groups:
        past_x = group // 2

        def ready(atom, dx, dy, dz, past_x=past_x, placed=placed):
            slot = past_x * SLOTS + atom
            copy_atom(own_upper, 0, 0, raw, slot, sems).wait()
            place(raw, slot, placed, atom, dy, dz)

        def work(atom, dx, dy, dz, past_x=past_x, placed=placed):
            sums = project(placed, atom, field, dx, dy, dz, past_x, 0)
            keep_sums(kept, past_x * SLOTS + atom, sums)

        for_atoms(meta, group, 0, 0, ready)
        for_atoms(meta, group, past_x, 0, work)
        sums_out[...] = pack(kept, past_x * SLOTS, meta[past_x, 48])


def ahead_kernel(
    meta, own, other, wave_ref, own_before, other_before, own_sums, other_sums,
    plain, field, kept, plain_sems,
):
    groups = ((0, own, own_before, own_sums), (2, other, other_before, other_sums))
    for copy in copy_front(wave_ref, plain, plain_sems):
        copy.start()
    clear_sums(kept, 2 * SLOTS)
    for copy in copy_front(wave_ref, plain, plain_sems):
        copy.wait()

    def tile_at(k, c, xb, y):
        if y >= BY - 1:
            return jnp.zeros((8, 128), f32)
        return plain[k, y, pl.ds(c * CELLS + xb * 8, 8), :]

    load_field(tile_at, field)
    for group, placed, before, sums_out in groups:

        def work(atom, dx, dy, dz, group=group, placed=placed):
            sums = project(placed, atom, field, dx, dy, dz, group // 2, 1)
            keep_sums(kept, group // 2 * SLOTS + atom, sums)

        for_atoms(meta, group, group // 2, 1, work)
        sums_out[...] = before[...] + pack(kept, group // 2 * SLOTS, meta[group // 2, 48])


def place_kernel(first, skip, meta, side, corner, side_placed, corner_placed, raw, sems):
    groups = ((1, side, side_placed), (3, corner, corner_placed))
    for group, ref, _ in groups:

        def begin(atom, dx, dy, dz, group=group, ref=ref):
            slot = group // 2 * HALF + atom - first
            copy_atom(ref, skip, atom - first, raw, slot, sems).start()

        for_atoms(meta, group, group // 2, 1, begin, first, HALF)
    for group, ref, placed in groups:

        def work(atom, dx, dy, dz, group=group, ref=ref, placed=placed):
            slot = group // 2 * HALF + atom - first
            copy_atom(ref, skip, atom - first, raw, slot, sems).wait()
            place(raw, slot, placed, atom - first, dy, dz)

        for_atoms(meta, group, group // 2, 1, work, first, HALF)


def spread_parts(meta, boxes, field, values):
    for (group, first, count), placed in zip(PARTS, boxes, strict=True):

        def work(atom, dx, dy, dz, group=group, first=first, placed=placed):
            scaled = unpack(values[group], atom)
            spread(placed, atom - first, field, scaled, dx, dy, dz, group // 2, group % 2)

        for_atoms(meta, group, group // 2, group % 2, work, first, count)


def second_kernel(meta, home, visit, coupling, *rest):
    boxes = rest[: len(PARTS)]
    scaled_out, low, high, field, kept = rest[len(PARTS) :]
    clear_field(field)
    clear_sums(kept, 4 * SLOTS)
    for group in range(4):
        matrix = coupling[row_of(group), pl.ds(0, 8), :]
        scaled_out[group] = couple((home, visit)[group % 2][group // 2], matrix)
    spread_parts(meta, boxes, field, scaled_out)
    clear_rims(field)
    for (group, first, count), placed in zip(PARTS, boxes, strict=True):

        def work(atom, dx, dy, dz, group=group, first=first, placed=placed):
            sums = project(placed, atom - first, field, dx, dy, dz, group // 2, group % 2)
            keep_sums(kept, group * SLOTS + atom, sums)

        for_atoms(meta, group, group // 2, group % 2, work, first, count)
    for group in range(4):
        packed = pack(kept, group * SLOTS, meta[row_of(group), 48])
        (low, high)[group // 2][group % 2] = packed


def last_kernel(meta, near, far, near_in, far_in, first_scaled, coupling, wave_ref, *rest):
    boxes = rest[: len(PARTS)]
    out, field, totals, plain, plain_sems = rest[len(PARTS) :]
    for copy in copy_plain(wave_ref, plain, plain_sems):
        copy.start()
    clear_field(field)
    row, lane = iotas()
    for group in range(4):
        at = group // 2
        if group % 2:
            coeffs = far[at] + far_in[at]
        else:
            coeffs = near[at] + near_in[at]
        second = couple(coeffs, coupling[row_of(group), pl.ds(0, 8), :])
        first = first_scaled[group]
        turned = jnp.where((row & 1) == 0, pltpu.roll(first, 7, 0), -pltpu.roll(first, 1, 0))
        totals[group] = time_step * turned - half_square * second
    spread_parts(meta, boxes, field, totals)
    for copy in copy_plain(wave_ref, plain, plain_sems):
        copy.wait()
    add_field(plain, field)
    backs = [
        pltpu.make_async_copy(plain.at[k], out.at[:, pl.ds(128 * k, 128)], plain_sems.at[k])
        for k in range(2)
    ]
    for copy in backs:
        copy.start()
    for copy in backs:
        copy.wait()


SMEM = pl.BlockSpec(memory_space=pltpu.SMEM)
VMEM = pl.BlockSpec(memory_space=pltpu.VMEM)
HBM = pl.BlockSpec(memory_space=pl.ANY)
params = pltpu.CompilerParams(vmem_limit_bytes=16 << 20)
cost = pl.CostEstimate(flops=20_000_000, bytes_accessed=16_000_000, transcendentals=0)
DMA = pltpu.SemaphoreType.DMA
small = jax.ShapeDtypeStruct((8, 128), f32)
pair_of = jax.ShapeDtypeStruct((2, 8, 128), f32)
plain_scratch = pltpu.VMEM((2, 4 * CELLS * CELLS, 128), f32)
front_scratch = pltpu.VMEM((2, BY - 1, 4 * CELLS, 128), f32)
field_scratch = pltpu.VMEM(FIELD, f32)


def tiles_scratch(slots):
    return pltpu.VMEM((slots, NP // 2, 8, 128), f32)


def raw_scratch(slots):
    return pltpu.VMEM((slots, ATOM_ROWS, 128), f32)


def placed_shape(slots):
    return jax.ShapeDtypeStruct((slots,) + PLACED, f32)


def call(body, name, out_shape, in_specs, out_specs, scratch):
    return pl.pallas_call(
        body,
        out_shape=out_shape,
        in_specs=in_specs,
        out_specs=out_specs,
        scratch_shapes=scratch,
        compiler_params=params,
        cost_estimate=cost,
        name=name,
    )


def near_coeffs(meta, own, other, wave):
    scratch = [raw_scratch(2 * SLOTS), plain_scratch, field_scratch, tiles_scratch(2 * SLOTS)]
    scratch += [DMA((2 * SLOTS,)), DMA((2,))]
    shapes = [placed_shape(SLOTS), placed_shape(SLOTS), small, small]
    run = call(near_kernel, "near_coeffs", shapes, [SMEM] + [HBM] * 5, [VMEM] * 4, scratch)
    return run(meta, *own, *other, wave)


def ahead_coeffs(meta, own, other, wave, own_before, other_before):
    scratch = [front_scratch, field_scratch, tiles_scratch(2 * SLOTS), DMA((2,))]
    specs = [SMEM, VMEM, VMEM, HBM, VMEM, VMEM]
    run = call(ahead_kernel, "ahead_coeffs", [small, small], specs, [VMEM] * 2, scratch)
    return run(meta, own, other, wave, own_before, other_before)


def place_behind(first, skip, meta, side, corner):
    scratch = [raw_scratch(2 * HALF), DMA((2 * HALF,))]
    shapes = [placed_shape(HALF), placed_shape(HALF)]
    body = functools.partial(place_kernel, first, skip)
    run = call(body, "place_behind", shapes, [SMEM, HBM, HBM], [VMEM] * 2, scratch)
    return run(meta, side, corner)


def second_coeffs(meta, home, visit, coupling, boxes):
    scratch = [field_scratch, tiles_scratch(4 * SLOTS)]
    shapes = [jax.ShapeDtypeStruct((4, 8, 128), f32), pair_of, pair_of]
    run = call(second_kernel, "second_coeffs", shapes, [SMEM] + [VMEM] * (3 + len(PARTS)), [VMEM] * 3, scratch)
    return run(meta, home, visit, coupling, *boxes)


def advance(meta, near, far, near_in, far_in, first_scaled, coupling, wave, boxes):
    scratch = [field_scratch, pltpu.VMEM((4, 8, 128), f32), plain_scratch, DMA((2,))]
    shape = jax.ShapeDtypeStruct(wave.shape, f32)
    specs = [SMEM] + [VMEM] * 6 + [HBM] + [VMEM] * len(PARTS)
    run = call(last_kernel, "advance", shape, specs, HBM, scratch)
    return run(meta, near, far, near_in, far_in, first_scaled, coupling, wave, *boxes)


def per_device(wave, atom_anchors, betas, couplings, atom_counts):
    plain = wave.reshape(4 * CELLS * CELLS, wave.shape[4])
    own = betas[0]

    front = wave.reshape(4 * CELLS, CELLS, wave.shape[4])[:, : BY - 1]
    ahead = shift(jnp.transpose(front, (1, 0, 2)), "gy", -1)

    here = jnp.stack([lax.axis_index("gx") * CELLS, lax.axis_index("gy") * CELLS, 0])
    offsets = atom_anchors[:, 0] - here[:, None].astype(jnp.int32)
    live = (jnp.arange(SLOTS) < atom_counts[0, 0]).astype(f32)
    turned = jnp.transpose(couplings[0] * live[:, None, None], (2, 0, 1)).reshape(NP, SLOTS * NP)
    numbers = jnp.concatenate([offsets.reshape(48), atom_counts.reshape(1), jnp.zeros((79,), jnp.int32)])
    message = jnp.concatenate([turned, numbers.astype(f32)[None]])
    sheet = jnp.pad(message, ((0, HEAD_ROWS - 9), (0, 0)))
    rows = jnp.transpose(own.reshape(SLOTS, NP, ATOM_ROWS // NP, 128), (0, 2, 1, 3)).reshape(-1, 128)
    half = HALF * ATOM_ROWS
    halves = [jnp.concatenate([sheet, rows[:half]]), rows[half:]]
    side = [shift(half, "gy", 1) for half in halves]
    other = [shift(half, "gx", 1) for half in halves]

    def sent(part):
        return part[:9]

    pair = jnp.stack([message, sent(other[0])])
    meta_pair = pair[:, 8].astype(jnp.int32)

    own_placed, other_placed, own_sums, other_sums = near_coeffs(meta_pair, halves, other, plain)
    lower, own_sums = lax.optimization_barrier((side[0], own_sums))
    corner_lower = shift(lower, "gx", 1)
    messages = jnp.concatenate([pair, sent(lower)[None], sent(corner_lower)[None]])
    meta = messages[:, 8].astype(jnp.int32)
    own_sums, other_sums = ahead_coeffs(meta_pair, own_placed, other_placed, ahead, own_sums, other_sums)
    home = jnp.stack([own_sums + shift(other_sums, "gx", -1), other_sums + shift(own_sums, "gx", 1)])
    upper, home = lax.optimization_barrier((side[1], home))
    corner_upper = shift(upper, "gx", 1)
    boxes = [own_placed, other_placed]
    boxes += place_behind(0, HEAD_ROWS, meta, lower, corner_lower)
    boxes += place_behind(HALF, 0, meta, upper, corner_upper)
    visit = shift(home, "gy", 1)

    first_scaled, low, high = second_coeffs(meta, home, visit, messages, boxes)
    low_in = shift(high, "gx", -1)
    high_in = shift(low, "gx", 1)
    low, high = low + low_in, high + high_in
    near = jnp.stack([low[0], high[0]])
    far = jnp.stack([low[1], high[1]])
    near_in = shift(far, "gy", -1)
    far_in = shift(near, "gy", 1)
    out = advance(meta, near, far, near_in, far_in, first_scaled, messages, plain, boxes)
    return out.reshape(wave.shape)


def solution(mesh):
    return jax.shard_map(
        per_device,
        mesh=mesh,
        in_specs=(
            P(None, None, "gx", "gy", None),
            P(None, "gx", "gy"),
            P("gx", "gy", None, None),
            P("gx", "gy", None, None),
            P("gx", "gy"),
        ),
        out_specs=P(None, None, "gx", "gy", None),
        check_vma=False,
    )
```

```python
import functools

import jax
import jax.numpy as jnp
from jax import lax
from jax.experimental import pallas as pl
from jax.experimental.pallas import tpu as pltpu
from jax.sharding import PartitionSpec as P

BX = 12
BY = 12
BZ = 16
NP = 8
SLOTS = 16
CELLS = 16
PAD = 3
ROWS = 72
HALF = SLOTS // 2
PARTS = ((0, 0, SLOTS), (2, 0, SLOTS), (1, 0, HALF), (3, 0, HALF), (1, HALF, HALF), (3, HALF, HALF))
time_step = 0.5
half_square = 0.5 * time_step * time_step
f32 = jnp.float32

FIELD = (2, (CELLS + 2 * PAD) * ROWS, 128)
PLACED = (BX, 2, NP, 128)
ATOM_ROWS = BX * BY * BZ * NP // 128
HEAD_ROWS = 16


def shift(block, axis, distance):
    n = lax.axis_size(axis)
    return lax.ppermute(block, axis, [(i, (i + distance) % n) for i in range(n)])


def iotas():
    row = lax.broadcasted_iota(jnp.int32, (8, 128), 0)
    lane = lax.broadcasted_iota(jnp.int32, (8, 128), 1)
    return row, lane


def exchange_blocks(tiles):
    row, lane = iotas()
    tiles = list(tiles)
    for d in (4, 2, 1):
        odd = (lane & (16 * d)) != 0
        for i in range(8):
            if i & d:
                continue
            a, b = tiles[i], tiles[i | d]
            tiles[i] = jnp.where(odd, pltpu.roll(b, 16 * d, 1), a)
            tiles[i | d] = jnp.where(odd, b, pltpu.roll(a, 128 - 16 * d, 1))
    return tiles


def field_rows(x, row):
    return pl.ds(x * ROWS + row, 8)


def load_field(tile_at, field):
    def part(step, carry):
        c, xb = step >> 1, step & 1
        for h in range(2):
            for k in range(2):
                tiles = [tile_at(k, c, xb, 8 * h + i) for i in range(8)]
                for i, tile in enumerate(exchange_blocks(tiles)):
                    start = (PAD + xb * 8) * ROWS + 32 * k + 4 * i + c
                    field[h, pl.ds(start, 8, stride=ROWS), :] = tile
        return carry

    lax.fori_loop(0, 8, part, 0)
    clear_rims(field)
    zero = jnp.zeros((8, 128), f32)
    for h in range(2):
        for x in range(CELLS):
            field[h, field_rows(PAD + x, 64), :] = zero


def add_field(plain, field):
    def part(step, carry):
        c, xb = step >> 1, step & 1
        for h in range(2):
            for k in range(2):
                tiles = [
                    field[h, pl.ds((PAD + xb * 8) * ROWS + 32 * k + 4 * i + c, 8, stride=ROWS), :]
                    for i in range(8)
                ]
                for i, tile in enumerate(exchange_blocks(tiles)):
                    at = pl.ds(c * 256 + xb * 128 + 8 * h + i, 8, stride=16)
                    plain[k, at, :] = plain[k, at, :] + tile
        return carry

    lax.fori_loop(0, 8, part, 0)


def clear_rims(field):
    zero = jnp.zeros((PAD * ROWS, 128), f32)
    for h in range(2):
        field[h, pl.ds(0, PAD * ROWS), :] = zero
        field[h, pl.ds((PAD + CELLS) * ROWS, PAD * ROWS), :] = zero


def clear_field(field):
    zero = jnp.zeros((ROWS, 128), f32)

    def plane(x, carry):
        for h in range(2):
            field[h, pl.ds(x * ROWS, ROWS), :] = zero
        return carry

    lax.fori_loop(0, CELLS + 2 * PAD, plane, 0)


def place(raw, raw_slot, placed, slot, dy, dz):
    row, lane = iotas()
    s = dz & 15
    amounts = {}
    for odd in range(2):
        for late in range(2):
            r = (dy * 16 + s - 16 * late - 64 * odd + 512) & 255
            q = r & 127
            flip = r > 127
            amounts[odd, late] = (q, jnp.logical_xor(lane < q, flip))
    keep = (lane & 15) >= s
    for u in range(BX):
        k = (3 * u) // 2
        a = raw[raw_slot, pl.ds(NP * k, NP), :]
        b = raw[raw_slot, pl.ds(NP * k + NP, NP), :]
        outs = []
        for late in range(2):
            q, from_b = amounts[u % 2, late]
            ra = pltpu.roll(a, q, 1)
            rb = pltpu.roll(b, q, 1)
            outs.append((jnp.where(from_b, rb, ra), jnp.where(from_b, ra, rb)))
        for h in range(2):
            placed[slot, u, h] = jnp.where(keep, outs[0][h], outs[1][h])


def masks(dy, dz, past_y):
    row, lane = iotas()
    s = dz & 15
    zl = lane & 15
    z_ok = jnp.logical_xor(zl < s, row < 4)
    result = []
    for h in range(2):
        y = (lane >> 4) + 8 * h
        if past_y:
            y_ok = y < dy + BY - CELLS
        else:
            y_ok = jnp.logical_and(y >= dy, y < dy + BY)
        result.append(jnp.logical_and(z_ok, y_ok))
    return result


def x_blocks(dx, past_x):
    if past_x:
        return (CELLS - dx) >> 2, 3, PAD + dx - CELLS
    return 0, jnp.minimum(3, (CELLS + 3 - dx) >> 2), PAD + dx


def project(placed, slot, field, dx, dy, dz, past_x, past_y):
    first, last, base = x_blocks(dx, past_x)
    mask = masks(dy, dz, past_y)
    rows = (dz >> 4) * 4

    def four(block, sums):
        sums = list(sums)
        for i in range(4):
            u = block * 4 + i
            for h in range(2):
                cells = field[h, field_rows(base + u, rows), :]
                cells = jnp.where(mask[h], cells, 0.0)
                for p in range(NP):
                    sums[p] = sums[p] + cells * placed[slot, u, h, pl.ds(p, 1), :]
        return tuple(sums)

    return lax.fori_loop(first, last, four, tuple(jnp.zeros((8, 128), f32) for _ in range(NP)))


def spread(placed, slot, field, scaled, dx, dy, dz, past_x, past_y):
    first, last, base = x_blocks(dx, past_x)
    mask = masks(dy, dz, past_y)
    rows = (dz >> 4) * 4

    def four(block, carry):
        at = [(i, h) for i in range(4) for h in range(2)]
        cells = [field[h, field_rows(base + block * 4 + i, rows), :] for i, h in at]
        sums = []
        for (i, h), old in zip(at, cells, strict=True):
            u = block * 4 + i
            total = scaled[0] * placed[slot, u, h, pl.ds(0, 1), :]
            for p in range(1, NP):
                total = total + scaled[p] * placed[slot, u, h, pl.ds(p, 1), :]
            sums.append(old + jnp.where(mask[h], total, 0.0))
        for (i, h), new in zip(at, sums, strict=True):
            field[h, field_rows(base + block * 4 + i, rows), :] = new
        return carry

    lax.fori_loop(first, last, four, 0)


def keep_sums(kept, slot, sums):
    row, lane = iotas()
    for q in range(NP // 2):
        even, odd = sums[2 * q], sums[2 * q + 1]
        other = pltpu.roll(jnp.where(row < 4, odd, even), 4, 0)
        kept[slot, q] = jnp.where(row < 4, even, odd) + other


def pack(kept, slot, count):
    row, lane = iotas()
    pair = jnp.where((lane & 1) == (row >> 2), lane >> 1, -1)

    def four(step, packed):
        for i in range(4):
            for q in range(NP // 2):
                value = jnp.sum(kept[slot + 4 * step + i, q], axis=1, keepdims=True)
                packed = jnp.where(pair == (4 * step + i) * (NP // 2) + q, value, packed)
        return packed

    return lax.fori_loop(0, (count + 3) >> 2, four, jnp.zeros((8, 128), f32))


def clear_sums(kept, slots):
    def one(slot, carry):
        kept[slot] = jnp.zeros((NP // 2, 8, 128), f32)
        return carry

    lax.fori_loop(0, slots, one, 0, unroll=2)


def unpack(scaled, atom):
    return [
        jnp.take_along_axis(
            scaled, jnp.full((8, 128), atom * NP + p, jnp.int32), axis=1, mode="promise_in_bounds"
        )
        for p in range(NP)
    ]


def couple(coeffs, turned):
    row, lane = iotas()
    whole = coeffs + pltpu.roll(coeffs, 4, 0)
    matrix = jnp.concatenate([jnp.where((lane >> 3) == a, turned, 0.0) for a in range(SLOTS)], axis=0)
    return jnp.dot(whole, matrix, precision=lax.Precision.HIGHEST, preferred_element_type=f32)


def row_of(group):
    return group % 2 * 2 + group // 2


def for_atoms(meta, group, past_x, past_y, body, first=0, count=SLOTS):
    at = row_of(group)
    stop = jnp.minimum(meta[at, 48], first + count)

    def one(atom, carry):
        dx, dy, dz = meta[at, atom], meta[at, 16 + atom], meta[at, 32 + atom]
        if not (past_x or past_y):
            body(atom, dx, dy, dz)
            return carry
        reach = dx > CELLS - BX if past_x else dy > CELLS - BY
        if past_x and past_y:
            reach = jnp.logical_and(reach, dy > CELLS - BY)

        @pl.when(reach)
        def _():
            body(atom, dx, dy, dz)

        return carry

    lax.fori_loop(first, stop, one, 0)


def copy_atom(ref, skip, local, into, slot, sems):
    rows = pl.ds(local * ATOM_ROWS + skip, ATOM_ROWS)
    return pltpu.make_async_copy(ref.at[rows], into.at[slot], sems.at[slot])


def copy_plain(wave_ref, plain, sems):
    return [
        pltpu.make_async_copy(wave_ref.at[:, pl.ds(128 * k, 128)], plain.at[k], sems.at[k])
        for k in range(2)
    ]


def copy_front(wave_ref, plain, sems):
    return [
        pltpu.make_async_copy(wave_ref.at[:, :, pl.ds(128 * k, 128)], plain.at[k], sems.at[k])
        for k in range(2)
    ]


def near_kernel(
    meta, own_lower, own_upper, lower, upper, wave_ref, own_placed, other_placed, own_sums, other_sums,
    raw, plain, field, kept, sems, plain_sems,
):
    groups = ((0, own_placed, own_sums), (2, other_placed, other_sums))
    for copy in copy_plain(wave_ref, plain, plain_sems):
        copy.start()
    for group, refs in ((0, (own_lower, own_upper)), (2, (lower, upper))):
        for first, skip, ref in ((0, HEAD_ROWS, refs[0]), (HALF, 0, refs[1])):

            def begin(atom, dx, dy, dz, group=group, first=first, skip=skip, ref=ref):
                slot = group // 2 * SLOTS + atom
                copy_atom(ref, skip, atom - first, raw, slot, sems).start()

            for_atoms(meta, group, 0, 0, begin, first, HALF)
    clear_sums(kept, 2 * SLOTS)
    for copy in copy_plain(wave_ref, plain, plain_sems):
        copy.wait()
    load_field(lambda k, c, xb, y: plain[k, pl.ds(c * 256 + xb * 128 + y, 8, stride=16), :], field)
    for group, placed, sums_out in groups:
        past_x = group // 2

        def ready(atom, dx, dy, dz, past_x=past_x, placed=placed):
            slot = past_x * SLOTS + atom
            copy_atom(own_upper, 0, 0, raw, slot, sems).wait()
            place(raw, slot, placed, atom, dy, dz)

        def work(atom, dx, dy, dz, past_x=past_x, placed=placed):
            sums = project(placed, atom, field, dx, dy, dz, past_x, 0)
            keep_sums(kept, past_x * SLOTS + atom, sums)

        for_atoms(meta, group, 0, 0, ready)
        for_atoms(meta, group, past_x, 0, work)
        sums_out[...] = pack(kept, past_x * SLOTS, meta[past_x, 48])


def ahead_kernel(
    meta, own, other, wave_ref, own_before, other_before, own_sums, other_sums,
    plain, field, kept, plain_sems,
):
    groups = ((0, own, own_before, own_sums), (2, other, other_before, other_sums))
    for copy in copy_front(wave_ref, plain, plain_sems):
        copy.start()
    clear_sums(kept, 2 * SLOTS)
    for copy in copy_front(wave_ref, plain, plain_sems):
        copy.wait()

    def tile_at(k, c, xb, y):
        if y >= BY - 1:
            return jnp.zeros((8, 128), f32)
        return plain[k, y, pl.ds(c * CELLS + xb * 8, 8), :]

    load_field(tile_at, field)
    for group, placed, before, sums_out in groups:

        def work(atom, dx, dy, dz, group=group, placed=placed):
            sums = project(placed, atom, field, dx, dy, dz, group // 2, 1)
            keep_sums(kept, group // 2 * SLOTS + atom, sums)

        for_atoms(meta, group, group // 2, 1, work)
        sums_out[...] = before[...] + pack(kept, group // 2 * SLOTS, meta[group // 2, 48])


def place_kernel(first, skip, meta, side, corner, side_placed, corner_placed, raw, sems):
    groups = ((1, side, side_placed), (3, corner, corner_placed))
    for group, ref, _ in groups:

        def begin(atom, dx, dy, dz, group=group, ref=ref):
            slot = group // 2 * HALF + atom - first
            copy_atom(ref, skip, atom - first, raw, slot, sems).start()

        for_atoms(meta, group, group // 2, 1, begin, first, HALF)
    for group, ref, placed in groups:

        def work(atom, dx, dy, dz, group=group, ref=ref, placed=placed):
            slot = group // 2 * HALF + atom - first
            copy_atom(ref, skip, atom - first, raw, slot, sems).wait()
            place(raw, slot, placed, atom - first, dy, dz)

        for_atoms(meta, group, group // 2, 1, work, first, HALF)


def spread_parts(meta, boxes, parts, field, values):
    for (group, first, count), placed in zip(parts, boxes, strict=True):

        def work(atom, dx, dy, dz, group=group, first=first, placed=placed):
            scaled = unpack(values[group], atom)
            spread(placed, atom - first, field, scaled, dx, dy, dz, group // 2, group % 2)

        for_atoms(meta, group, group // 2, group % 2, work, first, count)


def home_kernel(meta, home, coupling, own, other, field, scaled_out):
    clear_field(field)
    for at in range(2):
        scaled_out[at] = couple(home[at], coupling[at, pl.ds(0, 8), :])
    values = {0: scaled_out[0], 2: scaled_out[1]}
    spread_parts(meta, (own, other), PARTS[:2], field, values)


def second_kernel(meta, home_scaled, visit, coupling, *rest):
    boxes = rest[: len(PARTS)]
    _, scaled_out, low, high, field, kept = rest[len(PARTS) :]
    clear_sums(kept, 4 * SLOTS)
    for at in range(2):
        scaled_out[2 * at] = home_scaled[at]
        scaled_out[2 * at + 1] = couple(visit[at], coupling[2 + at, pl.ds(0, 8), :])
    spread_parts(meta, boxes[2:], PARTS[2:], field, scaled_out)
    clear_rims(field)
    for (group, first, count), placed in zip(PARTS, boxes, strict=True):

        def work(atom, dx, dy, dz, group=group, first=first, placed=placed):
            sums = project(placed, atom - first, field, dx, dy, dz, group // 2, group % 2)
            keep_sums(kept, group * SLOTS + atom, sums)

        for_atoms(meta, group, group // 2, group % 2, work, first, count)
    for group in range(4):
        packed = pack(kept, group * SLOTS, meta[row_of(group), 48])
        (low, high)[group // 2][group % 2] = packed


def last_kernel(meta, near, far, near_in, far_in, first_scaled, coupling, wave_ref, *rest):
    boxes = rest[: len(PARTS)]
    out, field, totals, plain, plain_sems = rest[len(PARTS) :]
    for copy in copy_plain(wave_ref, plain, plain_sems):
        copy.start()
    clear_field(field)
    row, lane = iotas()
    for group in range(4):
        at = group // 2
        if group % 2:
            coeffs = far[at] + far_in[at]
        else:
            coeffs = near[at] + near_in[at]
        second = couple(coeffs, coupling[row_of(group), pl.ds(0, 8), :])
        first = first_scaled[group]
        turned = jnp.where((row & 1) == 0, pltpu.roll(first, 7, 0), -pltpu.roll(first, 1, 0))
        totals[group] = time_step * turned - half_square * second
    spread_parts(meta, boxes, PARTS, field, totals)
    for copy in copy_plain(wave_ref, plain, plain_sems):
        copy.wait()
    add_field(plain, field)
    backs = [
        pltpu.make_async_copy(plain.at[k], out.at[:, pl.ds(128 * k, 128)], plain_sems.at[k])
        for k in range(2)
    ]
    for copy in backs:
        copy.start()
    for copy in backs:
        copy.wait()


SMEM = pl.BlockSpec(memory_space=pltpu.SMEM)
VMEM = pl.BlockSpec(memory_space=pltpu.VMEM)
HBM = pl.BlockSpec(memory_space=pl.ANY)
params = pltpu.CompilerParams(vmem_limit_bytes=16 << 20)
cost = pl.CostEstimate(flops=20_000_000, bytes_accessed=16_000_000, transcendentals=0)
DMA = pltpu.SemaphoreType.DMA
small = jax.ShapeDtypeStruct((8, 128), f32)
pair_of = jax.ShapeDtypeStruct((2, 8, 128), f32)
plain_scratch = pltpu.VMEM((2, 4 * CELLS * CELLS, 128), f32)
front_scratch = pltpu.VMEM((2, BY - 1, 4 * CELLS, 128), f32)
field_scratch = pltpu.VMEM(FIELD, f32)


def tiles_scratch(slots):
    return pltpu.VMEM((slots, NP // 2, 8, 128), f32)


def raw_scratch(slots):
    return pltpu.VMEM((slots, ATOM_ROWS, 128), f32)


def placed_shape(slots):
    return jax.ShapeDtypeStruct((slots,) + PLACED, f32)


def call(body, name, out_shape, in_specs, out_specs, scratch):
    return pl.pallas_call(
        body,
        out_shape=out_shape,
        in_specs=in_specs,
        out_specs=out_specs,
        scratch_shapes=scratch,
        compiler_params=params,
        cost_estimate=cost,
        name=name,
    )


def near_coeffs(meta, own, other, wave):
    scratch = [raw_scratch(2 * SLOTS), plain_scratch, field_scratch, tiles_scratch(2 * SLOTS)]
    scratch += [DMA((2 * SLOTS,)), DMA((2,))]
    shapes = [placed_shape(SLOTS), placed_shape(SLOTS), small, small]
    run = call(near_kernel, "near_coeffs", shapes, [SMEM] + [HBM] * 5, [VMEM] * 4, scratch)
    return run(meta, *own, *other, wave)


def ahead_coeffs(meta, own, other, wave, own_before, other_before):
    scratch = [front_scratch, field_scratch, tiles_scratch(2 * SLOTS), DMA((2,))]
    specs = [SMEM, VMEM, VMEM, HBM, VMEM, VMEM]
    run = call(ahead_kernel, "ahead_coeffs", [small, small], specs, [VMEM] * 2, scratch)
    return run(meta, own, other, wave, own_before, other_before)


def place_behind(first, skip, meta, side, corner):
    scratch = [raw_scratch(2 * HALF), DMA((2 * HALF,))]
    shapes = [placed_shape(HALF), placed_shape(HALF)]
    body = functools.partial(place_kernel, first, skip)
    run = call(body, "place_behind", shapes, [SMEM, HBM, HBM], [VMEM] * 2, scratch)
    return run(meta, side, corner)


def home_spread(meta, home, coupling, own, other):
    shapes = [jax.ShapeDtypeStruct(FIELD, f32), pair_of]
    run = call(home_kernel, "home_spread", shapes, [SMEM] + [VMEM] * 4, [VMEM] * 2, [])
    return run(meta, home, coupling, own, other)


def second_coeffs(meta, home_scaled, visit, coupling, boxes, field):
    n = len(PARTS)
    shapes = [jax.ShapeDtypeStruct((4, 8, 128), f32), pair_of, pair_of, jax.ShapeDtypeStruct(FIELD, f32)]
    run = pl.pallas_call(
        second_kernel,
        out_shape=shapes,
        in_specs=[SMEM] + [VMEM] * (4 + n),
        out_specs=[VMEM] * 4,
        scratch_shapes=[tiles_scratch(4 * SLOTS)],
        input_output_aliases={4 + n: 3},
        compiler_params=params,
        cost_estimate=cost,
        name="second_coeffs",
    )
    return run(meta, home_scaled, visit, coupling, *boxes, field)


def advance(meta, near, far, near_in, far_in, first_scaled, coupling, wave, boxes):
    scratch = [field_scratch, pltpu.VMEM((4, 8, 128), f32), plain_scratch, DMA((2,))]
    shape = jax.ShapeDtypeStruct(wave.shape, f32)
    specs = [SMEM] + [VMEM] * 6 + [HBM] + [VMEM] * len(PARTS)
    run = call(last_kernel, "advance", shape, specs, HBM, scratch)
    return run(meta, near, far, near_in, far_in, first_scaled, coupling, wave, *boxes)


def per_device(wave, atom_anchors, betas, couplings, atom_counts):
    plain = wave.reshape(4 * CELLS * CELLS, wave.shape[4])
    own = betas[0]

    front = wave.reshape(4 * CELLS, CELLS, wave.shape[4])[:, : BY - 1]
    ahead = shift(jnp.transpose(front, (1, 0, 2)), "gy", -1)

    here = jnp.stack([lax.axis_index("gx") * CELLS, lax.axis_index("gy") * CELLS, 0])
    offsets = atom_anchors[:, 0] - here[:, None].astype(jnp.int32)
    live = (jnp.arange(SLOTS) < atom_counts[0, 0]).astype(f32)
    turned = jnp.transpose(couplings[0] * live[:, None, None], (2, 0, 1)).reshape(NP, SLOTS * NP)
    numbers = jnp.concatenate([offsets.reshape(48), atom_counts.reshape(1), jnp.zeros((79,), jnp.int32)])
    message = jnp.concatenate([turned, numbers.astype(f32)[None]])
    sheet = jnp.pad(message, ((0, HEAD_ROWS - 9), (0, 0)))
    rows = jnp.transpose(own.reshape(SLOTS, NP, ATOM_ROWS // NP, 128), (0, 2, 1, 3)).reshape(-1, 128)
    half = HALF * ATOM_ROWS
    halves = [jnp.concatenate([sheet, rows[:half]]), rows[half:]]
    side = [shift(half, "gy", 1) for half in halves]
    other = [shift(half, "gx", 1) for half in halves]

    def sent(part):
        return part[:9]

    pair = jnp.stack([message, sent(other[0])])
    meta_pair = pair[:, 8].astype(jnp.int32)

    own_placed, other_placed, own_sums, other_sums = near_coeffs(meta_pair, halves, other, plain)
    lower, own_sums = lax.optimization_barrier((side[0], own_sums))
    corner_lower = shift(lower, "gx", 1)
    messages = jnp.concatenate([pair, sent(lower)[None], sent(corner_lower)[None]])
    meta = messages[:, 8].astype(jnp.int32)
    own_sums, other_sums = ahead_coeffs(meta_pair, own_placed, other_placed, ahead, own_sums, other_sums)
    home = jnp.stack([own_sums + shift(other_sums, "gx", -1), other_sums + shift(own_sums, "gx", 1)])
    upper, home = lax.optimization_barrier((side[1], home))
    corner_upper = shift(upper, "gx", 1)
    boxes = [own_placed, other_placed]
    boxes += place_behind(0, HEAD_ROWS, meta, lower, corner_lower)
    boxes += place_behind(HALF, 0, meta, upper, corner_upper)
    visit = shift(home, "gy", 1)
    field, home_scaled = home_spread(meta_pair, home, pair, own_placed, other_placed)

    first_scaled, low, high, _ = second_coeffs(meta, home_scaled, visit, messages, boxes, field)
    low_in = shift(high, "gx", -1)
    high_in = shift(low, "gx", 1)
    low, high = low + low_in, high + high_in
    near = jnp.stack([low[0], high[0]])
    far = jnp.stack([low[1], high[1]])
    near_in = shift(far, "gy", -1)
    far_in = shift(near, "gy", 1)
    out = advance(meta, near, far, near_in, far_in, first_scaled, messages, plain, boxes)
    return out.reshape(wave.shape)


def solution(mesh):
    return jax.shard_map(
        per_device,
        mesh=mesh,
        in_specs=(
            P(None, None, "gx", "gy", None),
            P(None, "gx", "gy"),
            P("gx", "gy", None, None),
            P("gx", "gy", None, None),
            P("gx", "gy"),
        ),
        out_specs=P(None, None, "gx", "gy", None),
        check_vma=False,
    )
```

```python
import functools

import jax
import jax.numpy as jnp
from jax import lax
from jax.experimental import pallas as pl
from jax.experimental.pallas import tpu as pltpu
from jax.sharding import PartitionSpec as P

BX = 12
BY = 12
BZ = 16
NP = 8
SLOTS = 16
CELLS = 16
PAD = 3
ROWS = 72
HALF = SLOTS // 2
PARTS = ((0, 0, SLOTS), (2, 0, SLOTS), (1, 0, HALF), (3, 0, HALF), (1, HALF, HALF), (3, HALF, HALF))
time_step = 0.5
half_square = 0.5 * time_step * time_step
f32 = jnp.float32

FIELD = (2, (CELLS + 2 * PAD) * ROWS, 128)
PLACED = (BX, 2, NP, 128)
ATOM_ROWS = BX * BY * BZ * NP // 128
HEAD_ROWS = 16


def shift(block, axis, distance):
    n = lax.axis_size(axis)
    return lax.ppermute(block, axis, [(i, (i + distance) % n) for i in range(n)])


def iotas():
    row = lax.broadcasted_iota(jnp.int32, (8, 128), 0)
    lane = lax.broadcasted_iota(jnp.int32, (8, 128), 1)
    return row, lane


def exchange_blocks(tiles):
    row, lane = iotas()
    tiles = list(tiles)
    for d in (4, 2, 1):
        odd = (lane & (16 * d)) != 0
        for i in range(8):
            if i & d:
                continue
            a, b = tiles[i], tiles[i | d]
            tiles[i] = jnp.where(odd, pltpu.roll(b, 16 * d, 1), a)
            tiles[i | d] = jnp.where(odd, b, pltpu.roll(a, 128 - 16 * d, 1))
    return tiles


def field_rows(x, row):
    return pl.ds(x * ROWS + row, 8)


def load_field(tile_at, field):
    def part(step, carry):
        c, xb = step >> 1, step & 1
        for h in range(2):
            for k in range(2):
                tiles = [tile_at(k, c, xb, 8 * h + i) for i in range(8)]
                for i, tile in enumerate(exchange_blocks(tiles)):
                    start = (PAD + xb * 8) * ROWS + 32 * k + 4 * i + c
                    field[h, pl.ds(start, 8, stride=ROWS), :] = tile
        return carry

    lax.fori_loop(0, 8, part, 0)
    clear_rims(field)
    zero = jnp.zeros((8, 128), f32)
    for h in range(2):
        for x in range(CELLS):
            field[h, field_rows(PAD + x, 64), :] = zero


def add_field(plain, field):
    def part(step, carry):
        c, xb = step >> 1, step & 1
        for h in range(2):
            for k in range(2):
                tiles = [
                    field[h, pl.ds((PAD + xb * 8) * ROWS + 32 * k + 4 * i + c, 8, stride=ROWS), :]
                    for i in range(8)
                ]
                for i, tile in enumerate(exchange_blocks(tiles)):
                    at = pl.ds(c * 256 + xb * 128 + 8 * h + i, 8, stride=16)
                    plain[k, at, :] = plain[k, at, :] + tile
        return carry

    lax.fori_loop(0, 8, part, 0)


def clear_rims(field):
    zero = jnp.zeros((PAD * ROWS, 128), f32)
    for h in range(2):
        field[h, pl.ds(0, PAD * ROWS), :] = zero
        field[h, pl.ds((PAD + CELLS) * ROWS, PAD * ROWS), :] = zero


def clear_field(field):
    zero = jnp.zeros((ROWS, 128), f32)

    def plane(x, carry):
        for h in range(2):
            field[h, pl.ds(x * ROWS, ROWS), :] = zero
        return carry

    lax.fori_loop(0, CELLS + 2 * PAD, plane, 0)


def place(raw, raw_slot, placed, slot, dy, dz):
    row, lane = iotas()
    s = dz & 15
    amounts = {}
    for odd in range(2):
        for late in range(2):
            r = (dy * 16 + s - 16 * late - 64 * odd + 512) & 255
            q = r & 127
            flip = r > 127
            amounts[odd, late] = (q, jnp.logical_xor(lane < q, flip))
    keep = (lane & 15) >= s
    for u in range(BX):
        k = (3 * u) // 2
        a = raw[raw_slot, pl.ds(NP * k, NP), :]
        b = raw[raw_slot, pl.ds(NP * k + NP, NP), :]
        outs = []
        for late in range(2):
            q, from_b = amounts[u % 2, late]
            ra = pltpu.roll(a, q, 1)
            rb = pltpu.roll(b, q, 1)
            outs.append((jnp.where(from_b, rb, ra), jnp.where(from_b, ra, rb)))
        for h in range(2):
            placed[slot, u, h] = jnp.where(keep, outs[0][h], outs[1][h])


def masks(dy, dz, past_y):
    row, lane = iotas()
    s = dz & 15
    zl = lane & 15
    z_ok = jnp.logical_xor(zl < s, row < 4)
    result = []
    for h in range(2):
        y = (lane >> 4) + 8 * h
        if past_y:
            y_ok = y < dy + BY - CELLS
        else:
            y_ok = jnp.logical_and(y >= dy, y < dy + BY)
        result.append(jnp.logical_and(z_ok, y_ok))
    return result


def x_blocks(dx, past_x):
    if past_x:
        return (CELLS - dx) >> 2, 3, PAD + dx - CELLS
    return 0, jnp.minimum(3, (CELLS + 3 - dx) >> 2), PAD + dx


def project(placed, slot, field, dx, dy, dz, past_x, past_y):
    first, last, base = x_blocks(dx, past_x)
    mask = masks(dy, dz, past_y)
    rows = (dz >> 4) * 4

    def four(block, sums):
        sums = list(sums)
        for i in range(4):
            u = block * 4 + i
            for h in range(2):
                cells = field[h, field_rows(base + u, rows), :]
                cells = jnp.where(mask[h], cells, 0.0)
                for p in range(NP):
                    sums[p] = sums[p] + cells * placed[slot, u, h, pl.ds(p, 1), :]
        return tuple(sums)

    return lax.fori_loop(first, last, four, tuple(jnp.zeros((8, 128), f32) for _ in range(NP)))


def spread(placed, slot, field, scaled, dx, dy, dz, past_x, past_y):
    first, last, base = x_blocks(dx, past_x)
    mask = masks(dy, dz, past_y)
    rows = (dz >> 4) * 4

    def four(block, carry):
        at = [(i, h) for i in range(4) for h in range(2)]
        cells = [field[h, field_rows(base + block * 4 + i, rows), :] for i, h in at]
        sums = []
        for (i, h), old in zip(at, cells, strict=True):
            u = block * 4 + i
            total = scaled[0] * placed[slot, u, h, pl.ds(0, 1), :]
            for p in range(1, NP):
                total = total + scaled[p] * placed[slot, u, h, pl.ds(p, 1), :]
            sums.append(old + jnp.where(mask[h], total, 0.0))
        for (i, h), new in zip(at, sums, strict=True):
            field[h, field_rows(base + block * 4 + i, rows), :] = new
        return carry

    lax.fori_loop(first, last, four, 0)


def keep_sums(kept, slot, sums):
    row, lane = iotas()
    for q in range(NP // 2):
        even, odd = sums[2 * q], sums[2 * q + 1]
        other = pltpu.roll(jnp.where(row < 4, odd, even), 4, 0)
        kept[slot, q] = jnp.where(row < 4, even, odd) + other


def pack(kept, slot, count):
    row, lane = iotas()
    pair = jnp.where((lane & 1) == (row >> 2), lane >> 1, -1)

    def four(step, packed):
        for i in range(4):
            for q in range(NP // 2):
                value = jnp.sum(kept[slot + 4 * step + i, q], axis=1, keepdims=True)
                packed = jnp.where(pair == (4 * step + i) * (NP // 2) + q, value, packed)
        return packed

    return lax.fori_loop(0, (count + 3) >> 2, four, jnp.zeros((8, 128), f32))


def clear_sums(kept, slots):
    def one(slot, carry):
        kept[slot] = jnp.zeros((NP // 2, 8, 128), f32)
        return carry

    lax.fori_loop(0, slots, one, 0, unroll=2)


def unpack(scaled, atom):
    return [
        jnp.take_along_axis(
            scaled, jnp.full((8, 128), atom * NP + p, jnp.int32), axis=1, mode="promise_in_bounds"
        )
        for p in range(NP)
    ]


def couple(coeffs, turned):
    row, lane = iotas()
    whole = coeffs + pltpu.roll(coeffs, 4, 0)
    matrix = jnp.concatenate([jnp.where((lane >> 3) == a, turned, 0.0) for a in range(SLOTS)], axis=0)
    return jnp.dot(whole, matrix, precision=lax.Precision.HIGHEST, preferred_element_type=f32)


def row_of(group):
    return group % 2 * 2 + group // 2


def for_atoms(meta, group, past_x, past_y, body, first=0, count=SLOTS):
    at = row_of(group)
    stop = jnp.minimum(meta[at, 48], first + count)

    def one(atom, carry):
        dx, dy, dz = meta[at, atom], meta[at, 16 + atom], meta[at, 32 + atom]
        if not (past_x or past_y):
            body(atom, dx, dy, dz)
            return carry
        reach = dx > CELLS - BX if past_x else dy > CELLS - BY
        if past_x and past_y:
            reach = jnp.logical_and(reach, dy > CELLS - BY)

        @pl.when(reach)
        def _():
            body(atom, dx, dy, dz)

        return carry

    lax.fori_loop(first, stop, one, 0)


def copy_atom(ref, skip, local, into, slot, sems):
    rows = pl.ds(local * ATOM_ROWS + skip, ATOM_ROWS)
    return pltpu.make_async_copy(ref.at[rows], into.at[slot], sems.at[slot])


def copy_plain(wave_ref, plain, sems):
    return [
        pltpu.make_async_copy(wave_ref.at[:, pl.ds(128 * k, 128)], plain.at[k], sems.at[k])
        for k in range(2)
    ]


def copy_front(wave_ref, plain, sems):
    return [
        pltpu.make_async_copy(wave_ref.at[:, :, pl.ds(128 * k, 128)], plain.at[k], sems.at[k])
        for k in range(2)
    ]


def near_kernel(
    meta, own_lower, own_upper, lower, upper, wave_ref, own_placed, other_placed, own_sums, other_sums,
    raw, plain, field, kept, sems, plain_sems,
):
    groups = ((0, own_placed, own_sums), (2, other_placed, other_sums))
    for copy in copy_plain(wave_ref, plain, plain_sems):
        copy.start()
    for group, refs in ((0, (own_lower, own_upper)), (2, (lower, upper))):
        for first, skip, ref in ((0, HEAD_ROWS, refs[0]), (HALF, 0, refs[1])):

            def begin(atom, dx, dy, dz, group=group, first=first, skip=skip, ref=ref):
                slot = group // 2 * SLOTS + atom
                copy_atom(ref, skip, atom - first, raw, slot, sems).start()

            for_atoms(meta, group, 0, 0, begin, first, HALF)
    clear_sums(kept, 2 * SLOTS)
    for copy in copy_plain(wave_ref, plain, plain_sems):
        copy.wait()
    load_field(lambda k, c, xb, y: plain[k, pl.ds(c * 256 + xb * 128 + y, 8, stride=16), :], field)
    for group, placed, sums_out in groups:
        past_x = group // 2

        def ready(atom, dx, dy, dz, past_x=past_x, placed=placed):
            slot = past_x * SLOTS + atom
            copy_atom(own_upper, 0, 0, raw, slot, sems).wait()
            place(raw, slot, placed, atom, dy, dz)

        def work(atom, dx, dy, dz, past_x=past_x, placed=placed):
            sums = project(placed, atom, field, dx, dy, dz, past_x, 0)
            keep_sums(kept, past_x * SLOTS + atom, sums)

        for_atoms(meta, group, 0, 0, ready)
        for_atoms(meta, group, past_x, 0, work)
        sums_out[...] = pack(kept, past_x * SLOTS, meta[past_x, 48])


def ahead_kernel(
    meta, own, other, wave_ref, own_before, other_before, own_sums, other_sums,
    plain, field, kept, plain_sems,
):
    groups = ((0, own, own_before, own_sums), (2, other, other_before, other_sums))
    for copy in copy_front(wave_ref, plain, plain_sems):
        copy.start()
    clear_sums(kept, 2 * SLOTS)
    for copy in copy_front(wave_ref, plain, plain_sems):
        copy.wait()

    def tile_at(k, c, xb, y):
        if y >= BY - 1:
            return jnp.zeros((8, 128), f32)
        return plain[k, y, pl.ds(c * CELLS + xb * 8, 8), :]

    load_field(tile_at, field)
    for group, placed, before, sums_out in groups:

        def work(atom, dx, dy, dz, group=group, placed=placed):
            sums = project(placed, atom, field, dx, dy, dz, group // 2, 1)
            keep_sums(kept, group // 2 * SLOTS + atom, sums)

        for_atoms(meta, group, group // 2, 1, work)
        sums_out[...] = before[...] + pack(kept, group // 2 * SLOTS, meta[group // 2, 48])


def place_kernel(first, skip, meta, side, corner, side_placed, corner_placed, raw, sems):
    groups = ((1, side, side_placed), (3, corner, corner_placed))
    for group, ref, _ in groups:

        def begin(atom, dx, dy, dz, group=group, ref=ref):
            slot = group // 2 * HALF + atom - first
            copy_atom(ref, skip, atom - first, raw, slot, sems).start()

        for_atoms(meta, group, group // 2, 1, begin, first, HALF)
    for group, ref, placed in groups:

        def work(atom, dx, dy, dz, group=group, ref=ref, placed=placed):
            slot = group // 2 * HALF + atom - first
            copy_atom(ref, skip, atom - first, raw, slot, sems).wait()
            place(raw, slot, placed, atom - first, dy, dz)

        for_atoms(meta, group, group // 2, 1, work, first, HALF)


def spread_parts(meta, boxes, parts, field, values):
    for (group, first, count), placed in zip(parts, boxes, strict=True):

        def work(atom, dx, dy, dz, group=group, first=first, placed=placed):
            scaled = unpack(values[group], atom)
            spread(placed, atom - first, field, scaled, dx, dy, dz, group // 2, group % 2)

        for_atoms(meta, group, group // 2, group % 2, work, first, count)


def home_kernel(meta, home, coupling, own, other, field, scaled_out):
    clear_field(field)
    for at in range(2):
        scaled_out[at] = couple(home[at], coupling[at, pl.ds(0, 8), :])
    values = {0: scaled_out[0], 2: scaled_out[1]}
    spread_parts(meta, (own, other), PARTS[:2], field, values)


def second_kernel(meta, home_scaled, visit, coupling, *rest):
    boxes = rest[: len(PARTS)]
    _, scaled_out, low, high, field, kept = rest[len(PARTS) :]
    clear_sums(kept, 4 * SLOTS)
    for at in range(2):
        scaled_out[2 * at] = home_scaled[at]
        scaled_out[2 * at + 1] = couple(visit[at], coupling[2 + at, pl.ds(0, 8), :])
    spread_parts(meta, boxes[2:], PARTS[2:], field, scaled_out)
    clear_rims(field)
    for (group, first, count), placed in zip(PARTS, boxes, strict=True):

        def work(atom, dx, dy, dz, group=group, first=first, placed=placed):
            sums = project(placed, atom - first, field, dx, dy, dz, group // 2, group % 2)
            keep_sums(kept, group * SLOTS + atom, sums)

        for_atoms(meta, group, group // 2, group % 2, work, first, count)
    for group in range(4):
        packed = pack(kept, group * SLOTS, meta[row_of(group), 48])
        (low, high)[group // 2][group % 2] = packed


def last_kernel(meta, near, far, near_in, far_in, first_scaled, coupling, wave_ref, *rest):
    boxes = rest[: len(PARTS)]
    out, field, totals, plain, plain_sems = rest[len(PARTS) :]
    for copy in copy_plain(wave_ref, plain, plain_sems):
        copy.start()
    clear_field(field)
    row, lane = iotas()
    for group in range(4):
        at = group // 2
        if group % 2:
            coeffs = far[at] + far_in[at]
        else:
            coeffs = near[at] + near_in[at]
        second = couple(coeffs, coupling[row_of(group), pl.ds(0, 8), :])
        first = first_scaled[group]
        turned = jnp.where((row & 1) == 0, pltpu.roll(first, 7, 0), -pltpu.roll(first, 1, 0))
        totals[group] = time_step * turned - half_square * second
    spread_parts(meta, boxes, PARTS, field, totals)
    for copy in copy_plain(wave_ref, plain, plain_sems):
        copy.wait()
    add_field(plain, field)
    backs = [
        pltpu.make_async_copy(plain.at[k], out.at[:, pl.ds(128 * k, 128)], plain_sems.at[k])
        for k in range(2)
    ]
    for copy in backs:
        copy.start()
    for copy in backs:
        copy.wait()


SMEM = pl.BlockSpec(memory_space=pltpu.SMEM)
VMEM = pl.BlockSpec(memory_space=pltpu.VMEM)
HBM = pl.BlockSpec(memory_space=pl.ANY)
params = pltpu.CompilerParams(vmem_limit_bytes=16 << 20)
cost = pl.CostEstimate(flops=20_000_000, bytes_accessed=16_000_000, transcendentals=0)
DMA = pltpu.SemaphoreType.DMA
small = jax.ShapeDtypeStruct((8, 128), f32)
pair_of = jax.ShapeDtypeStruct((2, 8, 128), f32)
plain_scratch = pltpu.VMEM((2, 4 * CELLS * CELLS, 128), f32)
front_scratch = pltpu.VMEM((2, BY - 1, 4 * CELLS, 128), f32)
field_scratch = pltpu.VMEM(FIELD, f32)


def tiles_scratch(slots):
    return pltpu.VMEM((slots, NP // 2, 8, 128), f32)


def raw_scratch(slots):
    return pltpu.VMEM((slots, ATOM_ROWS, 128), f32)


def placed_shape(slots):
    return jax.ShapeDtypeStruct((slots,) + PLACED, f32)


def call(body, name, out_shape, in_specs, out_specs, scratch):
    return pl.pallas_call(
        body,
        out_shape=out_shape,
        in_specs=in_specs,
        out_specs=out_specs,
        scratch_shapes=scratch,
        compiler_params=params,
        cost_estimate=cost,
        name=name,
    )


def near_coeffs(meta, own, other, wave):
    scratch = [raw_scratch(2 * SLOTS), plain_scratch, field_scratch, tiles_scratch(2 * SLOTS)]
    scratch += [DMA((2 * SLOTS,)), DMA((2,))]
    shapes = [placed_shape(SLOTS), placed_shape(SLOTS), small, small]
    run = call(near_kernel, "near_coeffs", shapes, [SMEM] + [HBM] * 5, [VMEM] * 4, scratch)
    return run(meta, *own, *other, wave)


def ahead_coeffs(meta, own, other, wave, own_before, other_before):
    scratch = [front_scratch, field_scratch, tiles_scratch(2 * SLOTS), DMA((2,))]
    specs = [SMEM, VMEM, VMEM, HBM, VMEM, VMEM]
    run = call(ahead_kernel, "ahead_coeffs", [small, small], specs, [VMEM] * 2, scratch)
    return run(meta, own, other, wave, own_before, other_before)


def place_behind(first, skip, meta, side, corner):
    scratch = [raw_scratch(2 * HALF), DMA((2 * HALF,))]
    shapes = [placed_shape(HALF), placed_shape(HALF)]
    body = functools.partial(place_kernel, first, skip)
    run = call(body, "place_behind", shapes, [SMEM, HBM, HBM], [VMEM] * 2, scratch)
    return run(meta, side, corner)


def home_spread(meta, home, coupling, own, other):
    shapes = [jax.ShapeDtypeStruct(FIELD, f32), pair_of]
    run = call(home_kernel, "home_spread", shapes, [SMEM] + [VMEM] * 4, [VMEM] * 2, [])
    return run(meta, home, coupling, own, other)


def second_coeffs(meta, home_scaled, visit, coupling, boxes, field):
    n = len(PARTS)
    shapes = [jax.ShapeDtypeStruct((4, 8, 128), f32), pair_of, pair_of, jax.ShapeDtypeStruct(FIELD, f32)]
    run = pl.pallas_call(
        second_kernel,
        out_shape=shapes,
        in_specs=[SMEM] + [VMEM] * (4 + n),
        out_specs=[VMEM] * 4,
        scratch_shapes=[tiles_scratch(4 * SLOTS)],
        input_output_aliases={4 + n: 3},
        compiler_params=params,
        cost_estimate=cost,
        name="second_coeffs",
    )
    return run(meta, home_scaled, visit, coupling, *boxes, field)


def advance(meta, near, far, near_in, far_in, first_scaled, coupling, wave, boxes):
    scratch = [field_scratch, pltpu.VMEM((4, 8, 128), f32), plain_scratch, DMA((2,))]
    shape = jax.ShapeDtypeStruct(wave.shape, f32)
    specs = [SMEM] + [VMEM] * 6 + [HBM] + [VMEM] * len(PARTS)
    run = call(last_kernel, "advance", shape, specs, HBM, scratch)
    return run(meta, near, far, near_in, far_in, first_scaled, coupling, wave, *boxes)


def per_device(wave, atom_anchors, betas, couplings, atom_counts):
    plain = wave.reshape(4 * CELLS * CELLS, wave.shape[4])
    own = betas[0]

    front = wave.reshape(4 * CELLS, CELLS, wave.shape[4])[:, : BY - 1]
    ahead = shift(jnp.transpose(front, (1, 0, 2)), "gy", -1)

    here = jnp.stack([lax.axis_index("gx") * CELLS, lax.axis_index("gy") * CELLS, 0])
    offsets = atom_anchors[:, 0] - here[:, None].astype(jnp.int32)
    live = (jnp.arange(SLOTS) < atom_counts[0, 0]).astype(f32)
    turned = jnp.transpose(couplings[0] * live[:, None, None], (2, 0, 1)).reshape(NP, SLOTS * NP)
    numbers = jnp.concatenate([offsets.reshape(48), atom_counts.reshape(1), jnp.zeros((79,), jnp.int32)])
    message = jnp.concatenate([turned, numbers.astype(f32)[None]])
    sheet = jnp.pad(message, ((0, HEAD_ROWS - 9), (0, 0)))
    rows = jnp.transpose(own.reshape(SLOTS, NP, ATOM_ROWS // NP, 128), (0, 2, 1, 3)).reshape(-1, 128)
    half = HALF * ATOM_ROWS
    halves = [jnp.concatenate([sheet, rows[:half]]), rows[half:]]
    side = [shift(half, "gy", 1) for half in halves]
    other = [shift(half, "gx", 1) for half in halves]

    def sent(part):
        return part[:9]

    pair = jnp.stack([message, sent(other[0])])
    meta_pair = pair[:, 8].astype(jnp.int32)

    own_placed, other_placed, own_sums, other_sums = near_coeffs(meta_pair, halves, other, plain)
    lower, own_sums = lax.optimization_barrier((side[0], own_sums))
    corner_lower = shift(lower, "gx", 1)
    messages = jnp.concatenate([pair, sent(lower)[None], sent(corner_lower)[None]])
    meta = messages[:, 8].astype(jnp.int32)
    own_sums, other_sums = ahead_coeffs(meta_pair, own_placed, other_placed, ahead, own_sums, other_sums)
    home = jnp.stack([own_sums + shift(other_sums, "gx", -1), other_sums + shift(own_sums, "gx", 1)])
    field, home_scaled = home_spread(meta_pair, home, pair, own_placed, other_placed)
    upper, home_scaled = lax.optimization_barrier((side[1], home_scaled))
    corner_upper = shift(upper, "gx", 1)
    boxes = [own_placed, other_placed]
    boxes += place_behind(0, HEAD_ROWS, meta, lower, corner_lower)
    boxes += place_behind(HALF, 0, meta, upper, corner_upper)
    visit = shift(home, "gy", 1)

    first_scaled, low, high, _ = second_coeffs(meta, home_scaled, visit, messages, boxes, field)
    low_in = shift(high, "gx", -1)
    high_in = shift(low, "gx", 1)
    low, high = low + low_in, high + high_in
    near = jnp.stack([low[0], high[0]])
    far = jnp.stack([low[1], high[1]])
    near_in = shift(far, "gy", -1)
    far_in = shift(near, "gy", 1)
    out = advance(meta, near, far, near_in, far_in, first_scaled, messages, plain, boxes)
    return out.reshape(wave.shape)


def solution(mesh):
    return jax.shard_map(
        per_device,
        mesh=mesh,
        in_specs=(
            P(None, None, "gx", "gy", None),
            P(None, "gx", "gy"),
            P("gx", "gy", None, None),
            P("gx", "gy", None, None),
            P("gx", "gy"),
        ),
        out_specs=P(None, None, "gx", "gy", None),
        check_vma=False,
    )
```
